256 devices in a mesh: rows: 32 (over x_hi, z, core), ch: 8 (over y, x_lo).
Axes of the slice: x: 4 (x_hi: 2, x_lo: 2; x = x_hi * 2 + x_lo), y: 4, z: 8, core: 2. Of those that a mesh axis runs over, the one named last changes fastest.
Arguments:
- fine_in: bfloat16 [48, 6144, 256], P(None, ('rows', 'ch')), may hold values from -6 to 6
- coarse_in: bfloat16 [96, 3072, 128], P('ch', 'rows'), may hold values from -6 to 6
- fine_kernel: bfloat16 [9, 48, 48], replicated, may hold values from -0.3125 to 0.3125
- coarse_kernel: bfloat16 [9, 96, 96], replicated, may hold values from -0.21875 to 0.21875
- up_weight: bfloat16 [48, 96], replicated, may hold values from -0.625 to 0.625
- down_weight: bfloat16 [9, 96, 48], replicated, may hold values from -0.3125 to 0.3125
- fine_cotangent: bfloat16 [48, 6144, 256], P(None, ('rows', 'ch')), may hold values from -6 to 6
- coarse_cotangent: bfloat16 [96, 3072, 128], P(None, ('rows', 'ch')), may hold values from -6 to 6
Outputs:
- joined_fine: bfloat16 [48, 6144, 256], P(None, ('rows', 'ch'))
- joined_coarse: bfloat16 [96, 3072, 128], P(None, ('rows', 'ch'))
- grad_up: float32 [48, 96], replicated
- grad_down: float32 [9, 96, 48], replicated
The draws below stay inside these ranges and needn't reach their ends.
All inputs are finite; a program needn't handle non-finite values.
Results may differ from the reference program's by a relative error of at most 0.025.
Values may be sent and summed in bfloat16 or wider, within the bound.
A program may use at most 128 MiB of HBM per device.

```python
import jax
import jax.numpy as jnp
from jax import lax

C1 = 48
C2 = 96
W1 = 256
H1 = 6144
H2 = 3072
W2 = 128


def block_scale(own_key, extent, shards, low, largest):
    gain = 1.0
    for axis_at, parts in shards:
        steps = jax.random.uniform(jax.random.fold_in(jax.random.fold_in(own_key, 6), axis_at), (parts,), jnp.float32, low / len(shards), largest / len(shards))
        gain = gain * jnp.repeat(jnp.exp(steps), extent[axis_at] // parts).reshape((-1,) + (1,) * (len(extent) - 1 - axis_at))
    return gain


def scatter_about(own_key, extent, scale, most, cuts=(), held_as=jnp.bfloat16):
    array = jax.random.normal(own_key, extent, jnp.float32) * scale
    if len(cuts) > 0:
        array = block_scale(own_key, extent, cuts, -0.22, 0.18) * array
    return jnp.clip(array, min=-most, max=most).astype(held_as)


def setup_inputs(seed: int = 0) -> dict:
    splits = jax.random.split(jax.random.key(seed), 9)
    return {
        "fine_in": scatter_about(splits[0], (C1, H1, W1), 1.0, 6.0, ((1, 256),)),
        "coarse_in": scatter_about(splits[1], (C2, H2, W2), 1.0, 6.0, ((0, 8), (1, 32))),
        "fine_kernel": scatter_about(splits[2], (9, C1, C1), (9 * C1) ** -0.5, 0.3125),
        "coarse_kernel": scatter_about(splits[3], (9, C2, C2), (9 * C2) ** -0.5, 0.21875),
        "up_weight": scatter_about(splits[4], (C1, C2), C2 ** -0.5, 0.625),
        "down_weight": scatter_about(splits[5], (9, C2, C1), (9 * C1) ** -0.5, 0.3125),
        "fine_cotangent": scatter_about(splits[6], (C1, H1, W1), 1.0, 6.0, ((1, 256),)),
        "coarse_cotangent": scatter_about(splits[7], (C2, H2, W2), 1.0, 6.0, ((1, 256),)),
    }


def smooth_gate(values):
    return jax.nn.gelu(values, approximate=True)

def kernel_layout(weight):
    shaped = weight.reshape(3, 3, weight.shape[1], weight.shape[2])
    return jnp.transpose(shaped, (2, 3, 0, 1))

def convolve(inputs, weight, stride, precision):
    result = lax.conv_general_dilated(inputs[None], kernel_layout(weight), (stride, stride), ((1, 1), (1, 1)), dimension_numbers=('NCHW', 'OIHW', 'NCHW'), precision=precision, preferred_element_type=jnp.float32)
    return result[0]

def reference(fine_in, coarse_in, fine_kernel, coarse_kernel, up_weight, down_weight, fine_cotangent, coarse_cotangent):
    features_fine = convolve(fine_in, fine_kernel, 1, None).astype(jnp.bfloat16)
    features_coarse = convolve(coarse_in, coarse_kernel, 1, None).astype(jnp.bfloat16)
    coarse_float = features_coarse.astype(jnp.float32)
    lifted = jnp.einsum('oc,chw->ohw', up_weight.astype(jnp.float32), coarse_float, precision=lax.Precision.HIGHEST)
    spread = jnp.repeat(jnp.repeat(lifted, 2, axis=1), 2, axis=2)
    pre_fine = features_fine.astype(jnp.float32) + spread
    joined_fine = smooth_gate(pre_fine).astype(jnp.bfloat16)
    fine_float = features_fine.astype(jnp.float32)

    def lower_with(kernel):
        return convolve(fine_float, kernel, 2, lax.Precision.HIGHEST)
    lowered, pull_kernel = jax.vjp(lower_with, down_weight.astype(jnp.float32))
    pre_coarse = coarse_float + lowered
    joined_coarse = smooth_gate(pre_coarse).astype(jnp.bfloat16)
    pullback_fine = jax.vjp(smooth_gate, pre_fine)[1]
    slope_fine = pullback_fine(fine_cotangent.astype(jnp.float32))[0].astype(jnp.bfloat16)
    pullback_coarse = jax.vjp(smooth_gate, pre_coarse)[1]
    slope_coarse = pullback_coarse(coarse_cotangent.astype(jnp.float32))[0].astype(jnp.bfloat16)
    channels = slope_fine.shape[0]
    pooled = slope_fine.astype(jnp.float32).reshape(channels, H2, 2, W2, 2).sum(axis=(2, 4)).astype(jnp.bfloat16)
    grad_up = jnp.einsum('ohw,chw->oc', pooled.astype(jnp.float32), coarse_float, precision=lax.Precision.HIGHEST)
    grad_down = pull_kernel(slope_coarse.astype(jnp.float32))[0]
    return (joined_fine, joined_coarse, grad_up, grad_down)
```

```python
import functools

import jax
import jax.numpy as jnp
from jax import lax
from jax.experimental import pallas as pl
from jax.experimental.pallas import tpu as pltpu
from jax.sharding import PartitionSpec as P

BF = jnp.bfloat16
F32 = jnp.float32
MESH = pl.DeviceIdType.MESH


def dot(a, b):
    return lax.dot_general(a, b, (((1,), (0,)), ((), ())), preferred_element_type=F32)


def dot_nt(a, b):
    return lax.dot_general(a, b, (((1,), (1,)), ((), ())), preferred_element_type=F32)


def one_hot(rows, cols, match):
    r = lax.broadcasted_iota(jnp.int32, (rows, cols), 0)
    c = lax.broadcasted_iota(jnp.int32, (rows, cols), 1)
    return jnp.where(match(r, c), 1.0, 0.0).astype(BF)


def split_columns():
    return one_hot(256, 512, lambda r, c: r == 2 * (c % 128) + c // 128 - 1)


def join_columns():
    return one_hot(256, 256, lambda r, c: c == 2 * (r % 128) + r // 128)


def gate(v):
    k, m = 0.7978845608028654, 0.044715
    q = v * v
    t = jnp.tanh(v * (k + (k * m) * q))
    half = 0.5 + 0.5 * t
    joined = v * half
    slope = half + (0.5 * v) * (1.0 - t * t) * (k + (3 * k * m) * q)
    return joined, slope


def prep_weights(fk, ck, dw, tb, wc, dm):
    fka = [fk[3 * a : 3 * a + 3].reshape(144, 48) for a in range(3)]
    for r in range(3):
        acc = None
        for a in range(3):
            d = dot(fka[a], one_hot(48, 240, lambda i, j: j == (r + a) * 48 + i))
            acc = d if acc is None else acc + d
        acc = acc.astype(BF)
        for b in range(3):
            tb[b, 48 * r : 48 * r + 48, :] = acc[48 * b : 48 * b + 48]
    place = one_hot(96, 128, lambda i, j: j == (i // 12) * 16 + i % 12)
    wide = dot(ck[...].reshape(864, 96), place).astype(BF)
    for t in range(9):
        a, b = t // 3, t % 3
        wc[96 * b : 96 * b + 96, 128 * a : 128 * a + 128] = wide[96 * t : 96 * t + 96]
    stacked = jnp.concatenate([dw[3 * a + b] for b in range(3) for a in range(3)], axis=0)
    dm[...] = stacked.T


def prep_coarse(ci, z):
    v = jnp.concatenate([ci[...], jnp.zeros((4, 96, 128), BF)], axis=0)
    z[1:97] = jnp.swapaxes(v, 0, 1)
    z[0] = jnp.zeros((16, 128), BF)
    z[97] = jnp.zeros((16, 128), BF)


def spread_fine(rows, u, at):
    n = rows.shape[0]
    u[at * 48 : (at + n) * 48, :] = dot(rows.reshape(n * 48, 256), split_columns()).astype(BF)


def store_features(g, at, out):
    lane = lax.broadcasted_iota(jnp.int32, (48, 128), 1)
    shifted = jnp.where(lane == 0, 0.0, pltpu.roll(out[:, 128:], 1, 1))
    g[at * 48 : at * 48 + 48, :] = jnp.concatenate([shifted, out], axis=1).astype(BF)


def fine_group(tb, u, g, group):
    acc = None
    base = (3 * group + 1) * 48
    for b in range(3):
        d = dot(tb[b], u[base : base + 240, 128 * b : 128 * b + 256])
        acc = d if acc is None else acc + d
    for r in range(3):
        store_features(g, 3 * group + r + 1, acc[48 * r : 48 * r + 48])


def fine_before(tb, u, g, keep):
    acc = None
    for b in range(3):
        d = dot(tb[b, 0:48, 0:144], u[0:144, 128 * b : 128 * b + 256])
        acc = d if acc is None else acc + d
    store_features(g, 0, jnp.where(keep, acc, 0.0))


def coarse_pair(wc, r, fc, p):
    i = 2 * p
    rows = jnp.concatenate(
        [r[i : i + 3].reshape(384, 128), r[i + 1 : i + 4].reshape(384, 128)], axis=1
    )
    y = dot(wc[...], rows)
    lane = lax.broadcasted_iota(jnp.int32, (96, 128), 1)
    for s in range(2):
        left = y[0:96, 128 * s : 128 * s + 128]
        mid = y[96:192, 128 * s : 128 * s + 128]
        right = y[192:288, 128 * s : 128 * s + 128]
        left = jnp.where(lane == 0, 0.0, pltpu.roll(left, 1, 1))
        right = jnp.where(lane == 127, 0.0, pltpu.roll(right, 127, 1))
        fc[p, :, 128 * s : 128 * s + 128] = (left + mid + right).astype(BF)


def windows(g, p):
    cols = []
    for i in (2 * p, 2 * p + 1):
        taps = [g[2 * i * 48 : (2 * i + 3) * 48, 128 * b : 128 * b + 128] for b in range(3)]
        cols.append(jnp.concatenate(taps, axis=0))
    return jnp.concatenate(cols, axis=1)


def join_pair(up, dm, g, fc, fcot, ccot, jf, jc, p):
    f = fc[p]
    lifted = dot(up[...], f)
    pooled = []
    for s in range(2):
        one = lifted[:, 128 * s : 128 * s + 128]
        both = jnp.concatenate([one, one], axis=1)
        total = None
        for a in range(2):
            h = 2 * (2 * p + s) + a
            pre = g[(h + 1) * 48 : (h + 2) * 48, 128:384].astype(F32) + both
            joined, slope = gate(pre)
            jf[h * 48 : (h + 1) * 48, :] = joined.astype(BF)
            term = (fcot[h * 48 : (h + 1) * 48, :].astype(F32) * slope).astype(BF).astype(F32)
            total = term if total is None else total + term
        pooled.append(total[:, :128] + total[:, 128:])
    pooled = jnp.concatenate(pooled, axis=1).astype(BF)
    gu = dot_nt(pooled, f)
    w = windows(g, p)
    pre = f.astype(F32) + dot(dm[...], w)
    joined, slope = gate(pre)
    for s in range(2):
        jc[2 * p + s] = joined[:, 128 * s : 128 * s + 128].astype(BF)
    cc = jnp.concatenate([ccot[2 * p], ccot[2 * p + 1]], axis=1).astype(F32)
    gd = dot_nt(w, (cc * slope).astype(BF))
    return gu, gd


def pack(gu, gd):
    rows = jnp.concatenate([gd, gu], axis=0)
    wide = jnp.concatenate([rows, jnp.zeros((480, 32), F32)], axis=1)
    tail = wide[384:480]
    lane = lax.broadcasted_iota(jnp.int32, (96, 128), 1)
    parts = []
    for k in range(4):
        head = wide[96 * k : 96 * k + 96]
        if k < 3:
            head = jnp.where(lane < 96, head, pltpu.roll(tail, 96 - 32 * k, 1))
        parts.append(head)
    return jnp.concatenate(parts, axis=0).reshape(16, 24, 128)


def unpack(total, grad_up, grad_down):
    flat = total.reshape(384, 128)
    lane = lax.broadcasted_iota(jnp.int32, (96, 128), 1)
    tail = None
    for k in range(3):
        moved = pltpu.roll(flat[96 * k : 96 * k + 96], (32 + 32 * k) % 128, 1)
        tail = moved if tail is None else jnp.where(lane < 32 * k, tail, moved)
    rows = jnp.concatenate([flat, tail], axis=0)[:, :96]
    for b in range(3):
        for a in range(3):
            k = 3 * b + a
            grad_down[3 * a + b] = rows[48 * k : 48 * k + 48]
    grad_up[...] = rows[432:480]


def kernel(
    nr, nc, x_h, ci_h, fk_h, ck_h, up_h, dw_h, fcot_h, ccot_h,
    jf_o, jc_o, gu_o, gd_o,
    x, ci, fk, ck, up, dw, fcot, ccot, in_sem, out_sem,
    tb, wc, dm, z, t, u, g, rr, fc, fct, jf, jft, jc, gu_v, gd_v,
    top, bot, hf, acc, s1, s2, s3,
    a2a_s, a2a_r, edge_s, edge_r, fine_s, fine_r, ar_s, ar_r,
):
    r = lax.axis_index("rows")
    c = lax.axis_index("ch")
    na = nr // 2
    nb = 2 * nc
    alpha = lax.rem(r, na)
    x_hi = r // na
    beta = x_hi * nc + c

    def in_a(d):
        k = lax.rem(alpha + d, na)
        return k, (x_hi * na + k, c)

    def in_b(d):
        k = lax.rem(beta + d, nb)
        return k, ((k // nc) * na + alpha, lax.rem(k, nc))

    loads = [
        pltpu.make_async_copy(src, dst, in_sem.at[k])
        for k, (src, dst) in enumerate(
            [(ci_h, ci), (x_h, x), (fk_h, fk), (ck_h, ck), (dw_h, dw), (up_h, up), (fcot_h, fcot), (ccot_h, ccot)]
        )
    ]
    for load in loads:
        load.start()

    barrier = pltpu.get_barrier_semaphore()

    def greet(device):
        pl.semaphore_signal(barrier, inc=1, device_id=device, device_id_type=MESH)

    @pl.loop(1, na)
    def _(d):
        greet(in_a(d)[1])

    @pl.loop(1, nb)
    def _(d):
        greet(in_b(d)[1])

    first_row, last_row = r == 0, r == nr - 1
    has_above, has_below = jnp.logical_not(first_row), jnp.logical_not(last_row)
    is_first = jnp.logical_and(c == 0, has_above)
    is_last = jnp.logical_and(c == nc - 1, has_below)

    @pl.when(has_below)
    def _():
        greet((r + 1, 0))

    @pl.when(has_above)
    def _():
        greet((r - 1, nc - 1))

    @pl.when(is_first)
    def _():
        @pl.loop(0, nc)
        def _(k):
            greet((r - 1, k))

    @pl.when(is_last)
    def _():
        @pl.loop(0, nc)
        def _(k):
            greet((r + 1, k))

    loads[0].wait()
    prep_coarse(ci, z)
    rr[:, pl.ds(c, 1)] = z[pl.ds(12 * c, 14)].reshape(14, 1, 16, 128)
    loads[1].wait()
    t[...] = jnp.swapaxes(x[...], 0, 1)

    one = jnp.int32(1)
    zero = jnp.int32(0)
    peers = na + nb - 2
    peers = peers + jnp.where(has_below, one, zero) + jnp.where(has_above, one, zero)
    peers = peers + jnp.where(is_first, nc * one, zero) + jnp.where(is_last, nc * one, zero)
    pl.semaphore_wait(barrier, peers)

    def a2a(d):
        peer = lax.rem(c + d, nc)
        return pltpu.make_async_remote_copy(
            src_ref=z.at[pl.ds(12 * peer, 14)],
            dst_ref=rr.at[:, c],
            send_sem=a2a_s.at[d],
            recv_sem=a2a_r.at[d],
            device_id=(r, peer),
            device_id_type=MESH,
        )

    @pl.loop(1, nc)
    def _(d):
        a2a(d).start()

    def edge(k, src, dst, device):
        return pltpu.make_async_remote_copy(
            src_ref=src, dst_ref=dst, send_sem=edge_s.at[k], recv_sem=edge_r.at[k, c],
            device_id=device, device_id_type=MESH,
        )

    edge_down = edge(0, z.at[96], top.at[c], (r + 1, 0))
    edge_up = edge(1, z.at[1], bot.at[c], (r - 1, nc - 1))

    @pl.when(has_below)
    def _():
        edge_down.start()

    @pl.when(has_above)
    def _():
        edge_up.start()

    wraps_down = c == nc - 1
    wraps_up = c == 0
    has_next = jnp.logical_not(jnp.logical_and(wraps_down, last_row))
    has_prev = jnp.logical_not(jnp.logical_and(wraps_up, first_row))
    next_dev = (r + jnp.where(wraps_down, one, zero), lax.rem(c + 1, nc))
    prev_dev = (r - jnp.where(wraps_up, one, zero), lax.rem(c + nc - 1, nc))

    def halo(k, src, dst, device):
        return pltpu.make_async_remote_copy(
            src_ref=src, dst_ref=dst, send_sem=fine_s.at[k], recv_sem=fine_r.at[k],
            device_id=device, device_id_type=MESH,
        )

    fine_down = halo(0, t.at[pl.ds(22, 2)], hf.at[pl.ds(0, 2)], next_dev)
    fine_up = halo(1, t.at[pl.ds(0, 1)], hf.at[pl.ds(2, 1)], prev_dev)

    @pl.when(has_next)
    def _():
        fine_down.start()

    @pl.when(has_prev)
    def _():
        fine_up.start()

    for load in loads[2:5]:
        load.wait()
    prep_weights(fk, ck, dw, tb, wc, dm)
    spread_fine(t[...], u, 2)
    for k in range(1, 7):
        fine_group(tb, u, g, k)
    for load in loads[5:]:
        load.wait()
    fct[...] = dot(
        jnp.swapaxes(fcot[...], 0, 1).reshape(1152, 256), split_columns()[:, 128:384]
    ).astype(BF)

    @pl.when(has_prev)
    def _():
        fine_down.wait_recv()
        spread_fine(hf[0:2], u, 0)

    @pl.when(jnp.logical_not(has_prev))
    def _():
        u[0:96, :] = jnp.zeros((96, 512), BF)

    @pl.when(has_next)
    def _():
        fine_up.wait_recv()
        spread_fine(hf[2:3], u, 26)

    @pl.when(jnp.logical_not(has_next))
    def _():
        u[26 * 48 : 27 * 48, :] = jnp.zeros((48, 512), BF)

    fine_before(tb, u, g, has_prev)
    fine_group(tb, u, g, 0)
    fine_group(tb, u, g, 7)

    @pl.loop(1, nc)
    def _(d):
        source = lax.rem(c - d + nc, nc)
        pltpu.make_async_remote_copy(
            src_ref=z.at[pl.ds(0, 14)],
            dst_ref=rr.at[:, source],
            send_sem=a2a_s.at[d],
            recv_sem=a2a_r.at[d],
            device_id=(r, source),
            device_id_type=MESH,
        ).wait_recv()

    def edge_wait(k, buf, row):
        @pl.loop(0, nc)
        def _(j):
            pltpu.make_async_remote_copy(
                src_ref=z.at[0], dst_ref=buf.at[j], send_sem=edge_s.at[k], recv_sem=edge_r.at[k, j],
                device_id=(r, c), device_id_type=MESH,
            ).wait_recv()

        rr[row] = buf[...]

    @pl.when(is_first)
    def _():
        edge_wait(0, top, 0)

    @pl.when(is_last)
    def _():
        edge_wait(1, bot, 13)

    for p in range(6):
        coarse_pair(wc, rr, fc, p)
    gu = gd = None
    for p in range(6):
        a, b = join_pair(up, dm, g, fc, fct, ccot, jf, jc, p)
        gu = a if gu is None else gu + a
        gd = b if gd is None else gd + b

    acc[...] = pack(gu, gd).astype(acc.dtype)

    def swap(stage, d, src, dst, device):
        return pltpu.make_async_remote_copy(
            src_ref=src, dst_ref=dst, send_sem=ar_s.at[stage, d], recv_sem=ar_r.at[stage, d],
            device_id=device, device_id_type=MESH,
        )

    @pl.loop(1, nb)
    def _(d):
        k, device = in_b(d)
        swap(0, d, acc.at[k], s1.at[d], device).start()

    stores = [pltpu.make_async_copy(jft, jf_o, out_sem.at[0]), pltpu.make_async_copy(jc, jc_o, out_sem.at[1])]
    stores[1].start()
    jft[...] = jnp.swapaxes(dot(jf[...], join_columns()).astype(BF).reshape(24, 48, 256), 0, 1)
    stores[0].start()

    @pl.loop(1, nb)
    def _(d):
        swap(0, d, acc.at[0], s1.at[d], (r, c)).wait_recv()

    part = acc[beta].astype(F32)
    for d in range(1, nb):
        part = part + s1[d].astype(F32)
    s2[alpha] = part.astype(s2.dtype)

    @pl.loop(1, na)
    def _(d):
        swap(1, d, s2.at[alpha], s2.at[alpha], in_a(d)[1]).start()

    @pl.loop(1, na)
    def _(d):
        k = lax.rem(alpha - d + na, na)
        swap(1, d, s2.at[alpha], s2.at[k], (r, c)).wait_recv()

    part = s2[0].astype(F32)
    for k in range(1, na):
        part = part + s2[k].astype(F32)
    s3[beta] = part.astype(s3.dtype)

    @pl.loop(1, nb)
    def _(d):
        swap(2, d, s3.at[beta], s3.at[beta], in_b(d)[1]).start()

    @pl.loop(1, nb)
    def _(d):
        k = lax.rem(beta - d + nb, nb)
        swap(2, d, s3.at[beta], s3.at[k], (r, c)).wait_recv()

    unpack(s3[...].astype(F32), gu_v, gd_v)
    grads = [pltpu.make_async_copy(gu_v, gu_o, out_sem.at[2]), pltpu.make_async_copy(gd_v, gd_o, out_sem.at[3])]
    for store in grads:
        store.start()

    @pl.loop(1, nc)
    def _(d):
        a2a(d).wait_send()

    @pl.when(has_below)
    def _():
        edge_down.wait_send()

    @pl.when(has_above)
    def _():
        edge_up.wait_send()

    @pl.when(has_next)
    def _():
        fine_down.wait_send()

    @pl.when(has_prev)
    def _():
        fine_up.wait_send()

    @pl.loop(1, nb)
    def _(d):
        k, device = in_b(d)
        swap(0, d, acc.at[k], s1.at[d], device).wait_send()
        swap(2, d, s3.at[beta], s3.at[beta], device).wait_send()

    @pl.loop(1, na)
    def _(d):
        swap(1, d, s2.at[alpha], s2.at[alpha], in_a(d)[1]).wait_send()

    for store in stores + grads:
        store.wait()


def shards(
    nr, nc, fine_in, coarse_in, fine_kernel, coarse_kernel, up_weight, down_weight, fine_cotangent, coarse_cotangent
):
    na, nb = nr // 2, 2 * nc
    vmem, dma = pltpu.VMEM, pltpu.SemaphoreType.DMA
    any_spec = pl.BlockSpec(memory_space=pl.ANY)
    joined_fine, joined_coarse, grad_up, grad_down = pl.pallas_call(
        functools.partial(kernel, nr, nc),
        out_shape=(
            jax.ShapeDtypeStruct((48, 24, 256), BF),
            jax.ShapeDtypeStruct((12, 96, 128), BF),
            jax.ShapeDtypeStruct((48, 96), F32),
            jax.ShapeDtypeStruct((9, 48, 96), F32),
        ),
        in_specs=[any_spec] * 8,
        out_specs=(any_spec,) * 4,
        scratch_shapes=[
            vmem((48, 24, 256), BF),
            vmem((12, 96, 128), BF),
            vmem((9, 48, 48), BF),
            vmem((9, 96, 96), BF),
            vmem((48, 96), BF),
            vmem((9, 48, 96), BF),
            vmem((48, 24, 256), BF),
            vmem((12, 96, 128), BF),
            dma((8,)),
            dma((4,)),
            vmem((3, 144, 240), BF),
            vmem((288, 384), BF),
            vmem((96, 432), BF),
            vmem((98, 16, 128), BF),
            vmem((24, 48, 256), BF),
            vmem((27 * 48, 512), BF),
            vmem((25 * 48, 384), BF),
            vmem((14, 8, 16, 128), BF),
            vmem((6, 96, 256), BF),
            vmem((1152, 256), BF),
            vmem((1152, 256), BF),
            vmem((48, 24, 256), BF),
            vmem((12, 96, 128), BF),
            vmem((48, 96), F32),
            vmem((9, 48, 96), F32),
            vmem((8, 16, 128), BF),
            vmem((8, 16, 128), BF),
            vmem((3, 48, 256), BF),
            vmem((nb, 24, 128), BF),
            vmem((nb, 24, 128), BF),
            vmem((na, 24, 128), BF),
            vmem((nb, 24, 128), BF),
            dma((nc,)),
            dma((nc,)),
            dma((2,)),
            dma((2, nc)),
            dma((2,)),
            dma((2,)),
            dma((3, max(na, nb))),
            dma((3, max(na, nb))),
        ],
        compiler_params=pltpu.CompilerParams(
            collective_id=0, has_side_effects=True, vmem_limit_bytes=40 << 20
        ),
    )(
        fine_in,
        coarse_in,
        fine_kernel,
        coarse_kernel,
        up_weight,
        jnp.swapaxes(down_weight, 1, 2),
        fine_cotangent,
        jnp.swapaxes(coarse_cotangent, 0, 1),
    )
    return joined_fine, jnp.swapaxes(joined_coarse, 0, 1), grad_up, jnp.swapaxes(grad_down, 1, 2)


def solution(mesh):
    strips = P(None, ("rows", "ch"), None)
    return jax.shard_map(
        functools.partial(shards, mesh.shape["rows"], mesh.shape["ch"]),
        mesh=mesh,
        in_specs=(strips, P("ch", "rows", None), P(), P(), P(), P(), strips, strips),
        out_specs=(strips, strips, P(), P()),
        check_vma=False,
    )
```

```python
import functools

import jax
import jax.numpy as jnp
from jax import lax
from jax.experimental import pallas as pl
from jax.experimental.pallas import tpu as pltpu
from jax.sharding import PartitionSpec as P

BF = jnp.bfloat16
F32 = jnp.float32
MESH = pl.DeviceIdType.MESH


def dot(a, b):
    return lax.dot_general(a, b, (((1,), (0,)), ((), ())), preferred_element_type=F32)


def dot_nt(a, b):
    return lax.dot_general(a, b, (((1,), (1,)), ((), ())), preferred_element_type=F32)


def one_hot(rows, cols, match):
    r = lax.broadcasted_iota(jnp.int32, (rows, cols), 0)
    c = lax.broadcasted_iota(jnp.int32, (rows, cols), 1)
    return jnp.where(match(r, c), 1.0, 0.0).astype(BF)


def split_columns():
    return one_hot(256, 512, lambda r, c: r == 2 * (c % 128) + c // 128 - 1)


def join_columns():
    return one_hot(256, 256, lambda r, c: c == 2 * (r % 128) + r // 128)


def gate(v):
    k, m = 0.7978845608028654, 0.044715
    q = v * v
    t = jnp.tanh(v * (k + (k * m) * q))
    half = 0.5 + 0.5 * t
    joined = v * half
    slope = half + (0.5 * v) * (1.0 - t * t) * (k + (3 * k * m) * q)
    return joined, slope


def prep_weights(fk, ck, dw, tb, wc, dm):
    fka = [fk[3 * a : 3 * a + 3].reshape(144, 48) for a in range(3)]
    for r in range(3):
        acc = None
        for a in range(3):
            d = dot(fka[a], one_hot(48, 240, lambda i, j: j == (r + a) * 48 + i))
            acc = d if acc is None else acc + d
        acc = acc.astype(BF)
        for b in range(3):
            tb[b, 48 * r : 48 * r + 48, :] = acc[48 * b : 48 * b + 48]
    place = one_hot(96, 128, lambda i, j: j == (i // 12) * 16 + i % 12)
    wide = dot(ck[...].reshape(864, 96), place).astype(BF)
    for t in range(9):
        a, b = t // 3, t % 3
        wc[96 * b : 96 * b + 96, 128 * a : 128 * a + 128] = wide[96 * t : 96 * t + 96]
    stacked = jnp.concatenate([dw[3 * a + b] for b in range(3) for a in range(3)], axis=0)
    dm[...] = stacked.T


def prep_coarse(ci, z):
    v = jnp.concatenate([ci[...], jnp.zeros((4, 96, 128), BF)], axis=0)
    z[1:97] = jnp.swapaxes(v, 0, 1)
    z[0] = jnp.zeros((16, 128), BF)
    z[97] = jnp.zeros((16, 128), BF)


def spread_fine(rows, u, at):
    n = rows.shape[0]
    u[at * 48 : (at + n) * 48, :] = dot(rows.reshape(n * 48, 256), split_columns()).astype(BF)


def store_features(g, at, out):
    lane = lax.broadcasted_iota(jnp.int32, (48, 128), 1)
    shifted = jnp.where(lane == 0, 0.0, pltpu.roll(out[:, 128:], 1, 1))
    g[at * 48 : at * 48 + 48, :] = jnp.concatenate([shifted, out], axis=1).astype(BF)


def fine_group(tb, u, g, group):
    acc = None
    base = (3 * group + 1) * 48
    for b in range(3):
        d = dot(tb[b], u[base : base + 240, 128 * b : 128 * b + 256])
        acc = d if acc is None else acc + d
    for r in range(3):
        store_features(g, 3 * group + r + 1, acc[48 * r : 48 * r + 48])


def fine_before(tb, u, g, keep):
    acc = None
    for b in range(3):
        d = dot(tb[b, 0:48, 0:144], u[0:144, 128 * b : 128 * b + 256])
        acc = d if acc is None else acc + d
    store_features(g, 0, jnp.where(keep, acc, 0.0))


def coarse_pair(wc, r, fc, p):
    i = 2 * p
    rows = jnp.concatenate(
        [r[i : i + 3].reshape(384, 128), r[i + 1 : i + 4].reshape(384, 128)], axis=1
    )
    y = dot(wc[...], rows)
    lane = lax.broadcasted_iota(jnp.int32, (96, 128), 1)
    for s in range(2):
        left = y[0:96, 128 * s : 128 * s + 128]
        mid = y[96:192, 128 * s : 128 * s + 128]
        right = y[192:288, 128 * s : 128 * s + 128]
        left = jnp.where(lane == 0, 0.0, pltpu.roll(left, 1, 1))
        right = jnp.where(lane == 127, 0.0, pltpu.roll(right, 127, 1))
        fc[p, :, 128 * s : 128 * s + 128] = (left + mid + right).astype(BF)


def windows(g, p):
    cols = []
    for i in (2 * p, 2 * p + 1):
        taps = [g[2 * i * 48 : (2 * i + 3) * 48, 128 * b : 128 * b + 128] for b in range(3)]
        cols.append(jnp.concatenate(taps, axis=0))
    return jnp.concatenate(cols, axis=1)


def join_pair(up, dm, g, fc, fcot, ccot, jf, jc, p):
    f = fc[p]
    lifted = dot(up[...], f)
    pooled = []
    for s in range(2):
        one = lifted[:, 128 * s : 128 * s + 128]
        both = jnp.concatenate([one, one], axis=1)
        total = None
        for a in range(2):
            h = 2 * (2 * p + s) + a
            pre = g[(h + 1) * 48 : (h + 2) * 48, 128:384].astype(F32) + both
            joined, slope = gate(pre)
            jf[h * 48 : (h + 1) * 48, :] = joined.astype(BF)
            term = (fcot[h * 48 : (h + 1) * 48, :].astype(F32) * slope).astype(BF).astype(F32)
            total = term if total is None else total + term
        pooled.append(total[:, :128] + total[:, 128:])
    pooled = jnp.concatenate(pooled, axis=1).astype(BF)
    gu = dot_nt(pooled, f)
    w = windows(g, p)
    pre = f.astype(F32) + dot(dm[...], w)
    joined, slope = gate(pre)
    for s in range(2):
        jc[2 * p + s] = joined[:, 128 * s : 128 * s + 128].astype(BF)
    cc = jnp.concatenate([ccot[2 * p], ccot[2 * p + 1]], axis=1).astype(F32)
    gd = dot_nt(w, (cc * slope).astype(BF))
    return gu, gd


def pack(gu, gd):
    rows = jnp.concatenate([gd, gu], axis=0)
    wide = jnp.concatenate([rows, jnp.zeros((480, 32), F32)], axis=1)
    tail = wide[384:480]
    lane = lax.broadcasted_iota(jnp.int32, (96, 128), 1)
    parts = []
    for k in range(4):
        head = wide[96 * k : 96 * k + 96]
        if k < 3:
            head = jnp.where(lane < 96, head, pltpu.roll(tail, 96 - 32 * k, 1))
        parts.append(head)
    return jnp.concatenate(parts, axis=0).reshape(16, 24, 128)


def unpack(total, grad_up, grad_down):
    flat = total.reshape(384, 128)
    lane = lax.broadcasted_iota(jnp.int32, (96, 128), 1)
    tail = None
    for k in range(3):
        moved = pltpu.roll(flat[96 * k : 96 * k + 96], (32 + 32 * k) % 128, 1)
        tail = moved if tail is None else jnp.where(lane < 32 * k, tail, moved)
    rows = jnp.concatenate([flat, tail], axis=0)[:, :96]
    for b in range(3):
        for a in range(3):
            k = 3 * b + a
            grad_down[3 * a + b] = rows[48 * k : 48 * k + 48]
    grad_up[...] = rows[432:480]


def kernel(
    nr, nc, x_h, ci_h, fk_h, ck_h, up_h, dw_h, fcot_h, ccot_h,
    jf_o, jc_o, gu_o, gd_o,
    x, ci, fk, ck, up, dw, fcot, ccot, in_sem, out_sem,
    tb, wc, dm, z, t, u, g, rr, fc, fct, jf, jft, jc, gu_v, gd_v,
    top, bot, hf, acc, s1, s2, s3,
    a2a_s, a2a_r, edge_s, edge_r, fine_s, fine_r, ar_s, ar_r,
):
    r = lax.axis_index("rows")
    c = lax.axis_index("ch")
    na = nr // 2
    nb = 2 * nc
    alpha = lax.rem(r, na)
    x_hi = r // na
    beta = x_hi * nc + c

    def in_a(d):
        k = lax.rem(alpha + d, na)
        return k, (x_hi * na + k, c)

    def in_b(d):
        k = lax.rem(beta + d, nb)
        return k, ((k // nc) * na + alpha, lax.rem(k, nc))

    loads = [
        pltpu.make_async_copy(src, dst, in_sem.at[k])
        for k, (src, dst) in enumerate(
            [(ci_h, ci), (x_h, x), (fk_h, fk), (ck_h, ck), (dw_h, dw), (up_h, up), (fcot_h, fcot), (ccot_h, ccot)]
        )
    ]
    for load in loads:
        load.start()

    barrier = pltpu.get_barrier_semaphore()

    def greet(device):
        pl.semaphore_signal(barrier, inc=1, device_id=device, device_id_type=MESH)

    @pl.loop(1, na)
    def _(d):
        greet(in_a(d)[1])

    @pl.loop(1, nb)
    def _(d):
        greet(in_b(d)[1])

    first_row, last_row = r == 0, r == nr - 1
    has_above, has_below = jnp.logical_not(first_row), jnp.logical_not(last_row)
    is_first = jnp.logical_and(c == 0, has_above)
    is_last = jnp.logical_and(c == nc - 1, has_below)

    @pl.when(has_below)
    def _():
        greet((r + 1, 0))

    @pl.when(has_above)
    def _():
        greet((r - 1, nc - 1))

    @pl.when(is_first)
    def _():
        @pl.loop(0, nc)
        def _(k):
            greet((r - 1, k))

    @pl.when(is_last)
    def _():
        @pl.loop(0, nc)
        def _(k):
            greet((r + 1, k))

    loads[0].wait()
    prep_coarse(ci, z)
    rr[:, pl.ds(c, 1)] = z[pl.ds(12 * c, 14)].reshape(14, 1, 16, 128)
    loads[1].wait()
    t[...] = jnp.swapaxes(x[...], 0, 1)

    one = jnp.int32(1)
    zero = jnp.int32(0)
    peers = na + nb - 2
    peers = peers + jnp.where(has_below, one, zero) + jnp.where(has_above, one, zero)
    peers = peers + jnp.where(is_first, nc * one, zero) + jnp.where(is_last, nc * one, zero)
    pl.semaphore_wait(barrier, peers)

    def a2a(d):
        peer = lax.rem(c + d, nc)
        return pltpu.make_async_remote_copy(
            src_ref=z.at[pl.ds(12 * peer, 14)],
            dst_ref=rr.at[:, c],
            send_sem=a2a_s.at[d],
            recv_sem=a2a_r.at[d],
            device_id=(r, peer),
            device_id_type=MESH,
        )

    @pl.loop(1, nc)
    def _(d):
        a2a(d).start()

    def edge(k, src, dst, device):
        return pltpu.make_async_remote_copy(
            src_ref=src, dst_ref=dst, send_sem=edge_s.at[k], recv_sem=edge_r.at[k, c],
            device_id=device, device_id_type=MESH,
        )

    edge_down = edge(0, z.at[96], top.at[c], (r + 1, 0))
    edge_up = edge(1, z.at[1], bot.at[c], (r - 1, nc - 1))

    @pl.when(has_below)
    def _():
        edge_down.start()

    @pl.when(has_above)
    def _():
        edge_up.start()

    wraps_down = c == nc - 1
    wraps_up = c == 0
    has_next = jnp.logical_not(jnp.logical_and(wraps_down, last_row))
    has_prev = jnp.logical_not(jnp.logical_and(wraps_up, first_row))
    next_dev = (r + jnp.where(wraps_down, one, zero), lax.rem(c + 1, nc))
    prev_dev = (r - jnp.where(wraps_up, one, zero), lax.rem(c + nc - 1, nc))

    def halo(k, src, dst, device):
        return pltpu.make_async_remote_copy(
            src_ref=src, dst_ref=dst, send_sem=fine_s.at[k], recv_sem=fine_r.at[k],
            device_id=device, device_id_type=MESH,
        )

    fine_down = halo(0, t.at[pl.ds(22, 2)], hf.at[pl.ds(0, 2)], next_dev)
    fine_up = halo(1, t.at[pl.ds(0, 1)], hf.at[pl.ds(2, 1)], prev_dev)

    @pl.when(has_next)
    def _():
        fine_down.start()

    @pl.when(has_prev)
    def _():
        fine_up.start()

    for load in loads[2:5]:
        load.wait()
    prep_weights(fk, ck, dw, tb, wc, dm)
    spread_fine(t[...], u, 2)
    for k in range(1, 7):
        fine_group(tb, u, g, k)
    for load in loads[5:]:
        load.wait()
    fct[...] = dot(
        jnp.swapaxes(fcot[...], 0, 1).reshape(1152, 256), split_columns()[:, 128:384]
    ).astype(BF)

    @pl.when(has_prev)
    def _():
        fine_down.wait_recv()
        spread_fine(hf[0:2], u, 0)

    @pl.when(jnp.logical_not(has_prev))
    def _():
        u[0:96, :] = jnp.zeros((96, 512), BF)

    @pl.when(has_next)
    def _():
        fine_up.wait_recv()
        spread_fine(hf[2:3], u, 26)

    @pl.when(jnp.logical_not(has_next))
    def _():
        u[26 * 48 : 27 * 48, :] = jnp.zeros((48, 512), BF)

    fine_before(tb, u, g, has_prev)
    fine_group(tb, u, g, 0)
    fine_group(tb, u, g, 7)

    @pl.loop(1, nc)
    def _(d):
        source = lax.rem(c - d + nc, nc)
        pltpu.make_async_remote_copy(
            src_ref=z.at[pl.ds(0, 14)],
            dst_ref=rr.at[:, source],
            send_sem=a2a_s.at[d],
            recv_sem=a2a_r.at[d],
            device_id=(r, source),
            device_id_type=MESH,
        ).wait_recv()

    def edge_wait(k, buf, row):
        @pl.loop(0, nc)
        def _(j):
            pltpu.make_async_remote_copy(
                src_ref=z.at[0], dst_ref=buf.at[j], send_sem=edge_s.at[k], recv_sem=edge_r.at[k, j],
                device_id=(r, c), device_id_type=MESH,
            ).wait_recv()

        rr[row] = buf[...]

    @pl.when(is_first)
    def _():
        edge_wait(0, top, 0)

    @pl.when(is_last)
    def _():
        edge_wait(1, bot, 13)

    for p in range(6):
        coarse_pair(wc, rr, fc, p)
    gu = gd = None
    for p in range(6):
        a, b = join_pair(up, dm, g, fc, fct, ccot, jf, jc, p)
        gu = a if gu is None else gu + a
        gd = b if gd is None else gd + b

    acc[...] = pack(gu, gd).astype(acc.dtype)

    def swap(stage, d, src, dst, device):
        return pltpu.make_async_remote_copy(
            src_ref=src, dst_ref=dst, send_sem=ar_s.at[stage, d], recv_sem=ar_r.at[stage, d],
            device_id=device, device_id_type=MESH,
        )

    @pl.loop(1, nb)
    def _(d):
        k, device = in_b(d)
        swap(0, d, acc.at[k], s1.at[d], device).start()

    stores = [pltpu.make_async_copy(jft, jf_o, out_sem.at[0]), pltpu.make_async_copy(jc, jc_o, out_sem.at[1])]
    stores[1].start()
    jft[...] = jnp.swapaxes(dot(jf[...], join_columns()).astype(BF).reshape(24, 48, 256), 0, 1)
    stores[0].start()

    @pl.loop(1, nb)
    def _(d):
        swap(0, d, acc.at[0], s1.at[d], (r, c)).wait_recv()

    part = acc[beta].astype(F32)
    for d in range(1, nb):
        part = part + s1[d].astype(F32)
    s2[alpha] = part.astype(s2.dtype)

    @pl.loop(1, na)
    def _(d):
        swap(1, d, s2.at[alpha], s2.at[alpha], in_a(d)[1]).start()

    @pl.loop(1, na)
    def _(d):
        k = lax.rem(alpha - d + na, na)
        swap(1, d, s2.at[alpha], s2.at[k], (r, c)).wait_recv()

    part = s2[0].astype(F32)
    for k in range(1, na):
        part = part + s2[k].astype(F32)
    s3[beta] = part.astype(s3.dtype)

    @pl.loop(1, nb)
    def _(d):
        swap(2, d, s3.at[beta], s3.at[beta], in_b(d)[1]).start()

    @pl.loop(1, nb)
    def _(d):
        k = lax.rem(beta - d + nb, nb)
        swap(2, d, s3.at[beta], s3.at[k], (r, c)).wait_recv()

    unpack(s3[...].astype(F32), gu_v, gd_v)
    grads = [pltpu.make_async_copy(gu_v, gu_o, out_sem.at[2]), pltpu.make_async_copy(gd_v, gd_o, out_sem.at[3])]
    for store in grads:
        store.start()

    @pl.loop(1, nc)
    def _(d):
        a2a(d).wait_send()

    @pl.when(has_below)
    def _():
        edge_down.wait_send()

    @pl.when(has_above)
    def _():
        edge_up.wait_send()

    @pl.when(has_next)
    def _():
        fine_down.wait_send()

    @pl.when(has_prev)
    def _():
        fine_up.wait_send()

    @pl.loop(1, nb)
    def _(d):
        k, device = in_b(d)
        swap(0, d, acc.at[k], s1.at[d], device).wait_send()
        swap(2, d, s3.at[beta], s3.at[beta], device).wait_send()

    @pl.loop(1, na)
    def _(d):
        swap(1, d, s2.at[alpha], s2.at[alpha], in_a(d)[1]).wait_send()

    for store in stores + grads:
        store.wait()


def write_out(*refs):
    sem = refs[8]
    copies = [pltpu.make_async_copy(refs[k], refs[4 + k], sem.at[k]) for k in range(4)]
    for copy in copies:
        copy.start()
    for copy in copies:
        copy.wait()


def shards(
    nr, nc, fine_in, coarse_in, fine_kernel, coarse_kernel, up_weight, down_weight, fine_cotangent, coarse_cotangent
):
    na, nb = nr // 2, 2 * nc
    vmem, dma = pltpu.VMEM, pltpu.SemaphoreType.DMA
    anywhere = pl.BlockSpec(memory_space=pl.ANY)
    shapes = [((48, 24, 256), BF), ((12, 96, 128), BF), ((48, 96), F32), ((9, 48, 96), F32)]
    results = pl.pallas_call(
        functools.partial(kernel, nr, nc),
        out_shape=tuple(vmem(*shape) for shape in shapes),
        in_specs=[anywhere] * 8,
        out_specs=(anywhere,) * 4,
        scratch_shapes=[
            vmem((48, 24, 256), BF),
            vmem((12, 96, 128), BF),
            vmem((9, 48, 48), BF),
            vmem((9, 96, 96), BF),
            vmem((48, 96), BF),
            vmem((9, 48, 96), BF),
            vmem((48, 24, 256), BF),
            vmem((12, 96, 128), BF),
            dma((8,)),
            dma((4,)),
            vmem((3, 144, 240), BF),
            vmem((288, 384), BF),
            vmem((96, 432), BF),
            vmem((98, 16, 128), BF),
            vmem((24, 48, 256), BF),
            vmem((27 * 48, 512), BF),
            vmem((25 * 48, 384), BF),
            vmem((14, 8, 16, 128), BF),
            vmem((6, 96, 256), BF),
            vmem((1152, 256), BF),
            vmem((1152, 256), BF),
            vmem((48, 24, 256), BF),
            vmem((12, 96, 128), BF),
            vmem((48, 96), F32),
            vmem((9, 48, 96), F32),
            vmem((8, 16, 128), BF),
            vmem((8, 16, 128), BF),
            vmem((3, 48, 256), BF),
            vmem((nb, 24, 128), BF),
            vmem((nb, 24, 128), BF),
            vmem((na, 24, 128), BF),
            vmem((nb, 24, 128), BF),
            dma((nc,)),
            dma((nc,)),
            dma((2,)),
            dma((2, nc)),
            dma((2,)),
            dma((2,)),
            dma((3, max(na, nb))),
            dma((3, max(na, nb))),
        ],
        compiler_params=pltpu.CompilerParams(
            collective_id=0, has_side_effects=True, vmem_limit_bytes=40 << 20
        ),
    )(
        *[
            pltpu.with_memory_space_constraint(array, pltpu.HBM)
            for array in (
                fine_in,
                coarse_in,
                fine_kernel,
                coarse_kernel,
                up_weight,
                jnp.swapaxes(down_weight, 1, 2),
                fine_cotangent,
                jnp.swapaxes(coarse_cotangent, 0, 1),
            )
        ]
    )
    joined_fine, joined_coarse, grad_up, grad_down = pl.pallas_call(
        write_out,
        out_shape=tuple(pltpu.HBM(*shape) for shape in shapes),
        in_specs=[anywhere] * 4,
        out_specs=(anywhere,) * 4,
        scratch_shapes=[dma((4,))],
    )(*[pltpu.with_memory_space_constraint(array, pltpu.VMEM) for array in results])
    return joined_fine, jnp.swapaxes(joined_coarse, 0, 1), grad_up, jnp.swapaxes(grad_down, 1, 2)


def solution(mesh):
    strips = P(None, ("rows", "ch"), None)
    return jax.shard_map(
        functools.partial(shards, mesh.shape["rows"], mesh.shape["ch"]),
        mesh=mesh,
        in_specs=(strips, P("ch", "rows", None), P(), P(), P(), P(), strips, strips),
        out_specs=(strips, strips, P(), P()),
        check_vma=False,
    )
```

```python
import functools

import jax
import jax.numpy as jnp
import numpy as np
from jax import lax
from jax.experimental import pallas as pl
from jax.experimental.pallas import tpu as pltpu
from jax.sharding import PartitionSpec as P

BF = jnp.bfloat16
F32 = jnp.float32
MESH = pl.DeviceIdType.MESH


def dot(a, b):
    return lax.dot_general(a, b, (((1,), (0,)), ((), ())), preferred_element_type=F32)


def dot_nt(a, b):
    return lax.dot_general(a, b, (((1,), (1,)), ((), ())), preferred_element_type=F32)


def one_hot(rows, cols, match):
    r = lax.broadcasted_iota(jnp.int32, (rows, cols), 0)
    c = lax.broadcasted_iota(jnp.int32, (rows, cols), 1)
    return jnp.where(match(r, c), 1.0, 0.0).astype(BF)


def split_columns():
    return one_hot(256, 512, lambda r, c: r == 2 * (c % 128) + c // 128 - 1)


def join_columns():
    return one_hot(256, 256, lambda r, c: c == 2 * (r % 128) + r // 128)


def gate(v):
    k, m = 0.7978845608028654, 0.044715
    q = v * v
    t = jnp.tanh(v * (k + (k * m) * q))
    half = 0.5 + 0.5 * t
    joined = v * half
    slope = half + (0.5 * v) * (1.0 - t * t) * (k + (3 * k * m) * q)
    return joined, slope


def prep_weights(fk, ck, dw, tb, wc, dm):
    fka = [fk[3 * a : 3 * a + 3].reshape(144, 48) for a in range(3)]
    for r in range(3):
        acc = None
        for a in range(3):
            d = dot(fka[a], one_hot(48, 240, lambda i, j: j == (r + a) * 48 + i))
            acc = d if acc is None else acc + d
        acc = acc.astype(BF)
        for b in range(3):
            tb[b, 48 * r : 48 * r + 48, :] = acc[48 * b : 48 * b + 48]
    place = one_hot(96, 128, lambda i, j: j == (i // 12) * 16 + i % 12)
    wide = dot(ck[...].reshape(864, 96), place).astype(BF)
    for t in range(9):
        a, b = t // 3, t % 3
        wc[96 * b : 96 * b + 96, 128 * a : 128 * a + 128] = wide[96 * t : 96 * t + 96]
    stacked = jnp.concatenate([dw[3 * a + b] for b in range(3) for a in range(3)], axis=0)
    dm[...] = stacked.T


def prep_coarse(ci, z):
    order = one_hot(192, 192, lambda r, k: k == (r % 12) * 16 + r // 12)
    for n in range(3):
        blocks = [ci[:, 16 * k : 16 * k + 16, :].reshape(192, 128) for k in (2 * n, 2 * n + 1)]
        out = dot(order, jnp.concatenate(blocks, axis=1)).astype(BF)
        for k in range(2):
            at = 16 + 192 * (2 * n + k)
            z[at : at + 192, :] = out[:, 128 * k : 128 * k + 128]
    z[0:16, :] = jnp.zeros((16, 128), BF)
    z[1168:1184, :] = jnp.zeros((16, 128), BF)


def place_part(slots, rr, part):
    (first, count), (row, rows) = PARTS[part], HEIGHTS[part]
    shift = 4 + 12 * row - first
    spread = one_hot(16 * rows, count, lambda r, k: (r % 16 < 12) & (k == shift + 12 * (r // 16) + r % 16))
    for n in range(4):
        both = [slots[k, first : first + count, :] for k in (2 * n, 2 * n + 1)]
        out = dot(spread, jnp.concatenate(both, axis=1)).astype(BF)
        for k in range(2):
            rr[row : row + rows, 2 * n + k] = out[:, 128 * k : 128 * k + 128].reshape(rows, 16, 128)


def spread_fine(rows, u, at):
    n = rows.shape[0]
    u[at * 48 : (at + n) * 48, :] = dot(rows.reshape(n * 48, 256), split_columns()).astype(BF)


def store_features(g, at, out):
    lane = lax.broadcasted_iota(jnp.int32, (48, 128), 1)
    shifted = jnp.where(lane == 0, 0.0, pltpu.roll(out[:, 128:], 1, 1))
    g[at * 48 : at * 48 + 48, :] = jnp.concatenate([shifted, out], axis=1).astype(BF)


def fine_group(tb, u, g, group):
    acc = None
    base = (3 * group + 1) * 48
    for b in range(3):
        d = dot(tb[b], u[base : base + 240, 128 * b : 128 * b + 256])
        acc = d if acc is None else acc + d
    for r in range(3):
        store_features(g, 3 * group + r + 1, acc[48 * r : 48 * r + 48])


def fine_before(tb, u, g, keep):
    acc = None
    for b in range(3):
        d = dot(tb[b, 0:48, 0:144], u[0:144, 128 * b : 128 * b + 256])
        acc = d if acc is None else acc + d
    store_features(g, 0, jnp.where(keep, acc, 0.0))


def coarse_pair(wc, rr, fc, p):
    i = 2 * p
    rows = jnp.concatenate(
        [rr[i : i + 3].reshape(384, 128), rr[i + 1 : i + 4].reshape(384, 128)], axis=1
    )
    y = dot(wc[...], rows)
    lane = lax.broadcasted_iota(jnp.int32, (96, 128), 1)
    for s in range(2):
        left = y[0:96, 128 * s : 128 * s + 128]
        mid = y[96:192, 128 * s : 128 * s + 128]
        right = y[192:288, 128 * s : 128 * s + 128]
        left = jnp.where(lane == 0, 0.0, pltpu.roll(left, 1, 1))
        right = jnp.where(lane == 127, 0.0, pltpu.roll(right, 127, 1))
        fc[p, :, 128 * s : 128 * s + 128] = (left + mid + right).astype(BF)


def windows(g, p):
    cols = []
    for i in (2 * p, 2 * p + 1):
        taps = [g[2 * i * 48 : (2 * i + 3) * 48, 128 * b : 128 * b + 128] for b in range(3)]
        cols.append(jnp.concatenate(taps, axis=0))
    return jnp.concatenate(cols, axis=1)


def join_pair(up, dm, g, fc, fcot, ccot, jf, jc, p):
    f = fc[p]
    lifted = dot(up[...], f)
    pooled = []
    for s in range(2):
        one = lifted[:, 128 * s : 128 * s + 128]
        both = jnp.concatenate([one, one], axis=1)
        total = None
        for a in range(2):
            h = 2 * (2 * p + s) + a
            pre = g[(h + 1) * 48 : (h + 2) * 48, 128:384].astype(F32) + both
            joined, slope = gate(pre)
            jf[h * 48 : (h + 1) * 48, :] = joined.astype(BF)
            term = (fcot[h * 48 : (h + 1) * 48, :].astype(F32) * slope).astype(BF).astype(F32)
            total = term if total is None else total + term
        pooled.append(total[:, :128] + total[:, 128:])
    pooled = jnp.concatenate(pooled, axis=1).astype(BF)
    gu = dot_nt(pooled, f)
    w = windows(g, p)
    pre = f.astype(F32) + dot(dm[...], w)
    joined, slope = gate(pre)
    for s in range(2):
        jc[2 * p + s] = joined[:, 128 * s : 128 * s + 128].astype(BF)
    cc = jnp.concatenate([ccot[2 * p], ccot[2 * p + 1]], axis=1).astype(F32)
    gd = dot_nt(w, (cc * slope).astype(BF))
    return gu, gd


def pack(gu, gd):
    rows = jnp.concatenate([gd, gu], axis=0)
    wide = jnp.concatenate([rows, jnp.zeros((480, 32), F32)], axis=1)
    tail = wide[384:480]
    lane = lax.broadcasted_iota(jnp.int32, (96, 128), 1)
    parts = []
    for k in range(4):
        head = wide[96 * k : 96 * k + 96]
        if k < 3:
            head = jnp.where(lane < 96, head, pltpu.roll(tail, 96 - 32 * k, 1))
        parts.append(head)
    return jnp.concatenate(parts, axis=0).reshape(16, 24, 128)


def unpack(total, grad_up, grad_down):
    flat = total.reshape(384, 128)
    lane = lax.broadcasted_iota(jnp.int32, (96, 128), 1)
    tail = None
    for k in range(3):
        moved = pltpu.roll(flat[96 * k : 96 * k + 96], (32 + 32 * k) % 128, 1)
        tail = moved if tail is None else jnp.where(lane < 32 * k, tail, moved)
    rows = jnp.concatenate([flat, tail], axis=0)[:, :96]
    for b in range(3):
        for a in range(3):
            k = 3 * b + a
            grad_down[3 * a + b] = rows[48 * k : 48 * k + 48]
    grad_up[...] = rows[432:480]


def farthest_first(sizes):
    def hops(digits):
        total = 0
        for name, step in zip(sizes, digits):
            if name == "core":
                total += 0.1 * step
            elif name == "x_hi":
                total += 2 * step
            elif name == "x_lo":
                total += step
            else:
                total += min(step, sizes[name] - step)
        return total

    every = [digits for digits in np.ndindex(*sizes.values()) if any(digits)]
    return sorted(every, key=lambda digits: -hops(digits))


SIZES = {"x_hi": 2, "z": 8, "core": 2, "y": 4, "x_lo": 2}
GROUP_A = {name: SIZES[name] for name in ("z", "core")}
GROUP_B = {name: SIZES[name] for name in ("x_hi", "y", "x_lo")}
GROUP_C = {name: SIZES[name] for name in ("y", "x_lo")}
ORDER_A, ORDER_B, ORDER_C = [farthest_first(group) for group in (GROUP_A, GROUP_B, GROUP_C)]
NR, NC, NA, NB = 32, 8, 16, 16
PARTS = ((0, 112), (112, 64))
HEIGHTS = ((0, 9), (9, 5))


def kernel(
    x_h, ci_h, fk_h, ck_h, up_h, dw_h, fcot_h, ccot_h,
    jf_o, jc_o, gu_o, gd_o,
    x, ci, fk, ck, up, dw, fcot, ccot, in_sem, out_sem,
    tb, wc, dm, z, t, u, g, slots, rr, fc, fct, jf, jft, jc, gu_v, gd_v,
    top, bot, hf, acc, s1, s2, s3,
    a2a_s, a2a_r, edge_s, edge_r, fine_s, fine_r, ar_s, ar_r,
):
    loads = [
        pltpu.make_async_copy(src, dst, in_sem.at[k])
        for k, (src, dst) in enumerate(
            [(ci_h, ci), (x_h, x), (fk_h, fk), (ck_h, ck), (dw_h, dw), (up_h, up), (fcot_h, fcot), (ccot_h, ccot)]
        )
    ]
    for load in loads:
        load.start()

    r = lax.axis_index("rows")
    c = lax.axis_index("ch")
    alpha = lax.rem(r, NA)
    x_hi = r // NA
    beta = x_hi * NC + c
    here = {"x_hi": x_hi, "z": alpha // 2, "core": lax.rem(r, 2), "y": c // 2, "x_lo": lax.rem(c, 2)}

    def member(group, digits, sign):
        at = dict(here)
        for name, step in zip(group, digits):
            if step:
                step = step if sign > 0 else SIZES[name] - step
                at[name] = lax.rem(at[name] + step, SIZES[name])
        a = at["z"] * 2 + at["core"]
        ch = at["y"] * 2 + at["x_lo"]
        return a, at["x_hi"] * NC + ch, (at["x_hi"] * NA + a, ch)

    ahead_a = [member(GROUP_A, digits, 1) for digits in ORDER_A]
    ahead_b = [member(GROUP_B, digits, 1) for digits in ORDER_B]
    ahead_c = [member(GROUP_C, digits, 1) for digits in ORDER_C]
    back_a = [member(GROUP_A, digits, -1) for digits in ORDER_A]
    back_b = [member(GROUP_B, digits, -1) for digits in ORDER_B]
    back_c = [member(GROUP_C, digits, -1) for digits in ORDER_C]

    barrier = pltpu.get_barrier_semaphore()

    def greet(device):
        pl.semaphore_signal(barrier, inc=1, device_id=device, device_id_type=MESH)

    first_row, last_row = r == 0, r == NR - 1
    has_above, has_below = jnp.logical_not(first_row), jnp.logical_not(last_row)
    is_first = jnp.logical_and(c == 0, has_above)
    is_last = jnp.logical_and(c == NC - 1, has_below)

    for _, _, device in ahead_b:
        greet(device)

    @pl.when(has_below)
    def _():
        greet((r + 1, 0))

    @pl.when(has_above)
    def _():
        greet((r - 1, NC - 1))

    @pl.when(is_first)
    def _():
        for k in range(NC):
            greet((r - 1, k))

    @pl.when(is_last)
    def _():
        for k in range(NC):
            greet((r + 1, k))

    for _, _, device in ahead_a:
        greet(device)

    loads[0].wait()
    prep_coarse(ci, z)

    one = jnp.int32(1)
    zero = jnp.int32(0)
    peers = NA + NB - 2
    peers = peers + jnp.where(has_below, one, zero) + jnp.where(has_above, one, zero)
    peers = peers + jnp.where(is_first, NC * one, zero) + jnp.where(is_last, NC * one, zero)
    pl.semaphore_wait(barrier, peers)

    def a2a(part, n, row, slot, device):
        first, count = PARTS[part]
        return pltpu.make_async_remote_copy(
            src_ref=z.at[pl.ds(pl.multiple_of(144 * row + first, 16), count)],
            dst_ref=slots.at[slot, pl.ds(first, count)],
            send_sem=a2a_s.at[part, n],
            recv_sem=a2a_r.at[part, n],
            device_id=device,
            device_id_type=MESH,
        )

    sends = [
        a2a(part, n, device[1], c, device) for part in range(2) for n, (_, _, device) in enumerate(ahead_c)
    ]
    for copy in sends[:7]:
        copy.start()

    def edge(k, src, dst, device):
        return pltpu.make_async_remote_copy(
            src_ref=src, dst_ref=dst, send_sem=edge_s.at[k], recv_sem=edge_r.at[k, c],
            device_id=device, device_id_type=MESH,
        )

    edge_down = edge(0, z.at[pl.ds(1152, 16)], top.at[c], (r + 1, 0))
    edge_up = edge(1, z.at[pl.ds(16, 16)], bot.at[c], (r - 1, NC - 1))

    @pl.when(has_below)
    def _():
        edge_down.start()

    @pl.when(has_above)
    def _():
        edge_up.start()

    wraps_down = c == NC - 1
    wraps_up = c == 0
    has_next = jnp.logical_not(jnp.logical_and(wraps_down, last_row))
    has_prev = jnp.logical_not(jnp.logical_and(wraps_up, first_row))
    next_dev = (r + jnp.where(wraps_down, one, zero), lax.rem(c + 1, NC))
    prev_dev = (r - jnp.where(wraps_up, one, zero), lax.rem(c + NC - 1, NC))

    def halo(k, src, dst, device):
        return pltpu.make_async_remote_copy(
            src_ref=src, dst_ref=dst, send_sem=fine_s.at[k], recv_sem=fine_r.at[k],
            device_id=device, device_id_type=MESH,
        )

    loads[1].wait()
    t[...] = jnp.swapaxes(x[...], 0, 1)
    fine_down = halo(0, t.at[pl.ds(22, 2)], hf.at[pl.ds(0, 2)], next_dev)
    fine_up = halo(1, t.at[pl.ds(0, 1)], hf.at[pl.ds(2, 1)], prev_dev)

    @pl.when(has_next)
    def _():
        fine_down.start()

    @pl.when(has_prev)
    def _():
        fine_up.start()

    for copy in sends[7:]:
        copy.start()
    slots[pl.ds(c, 1)] = z[pl.ds(pl.multiple_of(144 * c, 16), 176), :].reshape(1, 176, 128)

    for load in loads[2:5]:
        load.wait()
    prep_weights(fk, ck, dw, tb, wc, dm)
    spread_fine(t[...], u, 2)
    for k in range(1, 7):
        fine_group(tb, u, g, k)
    for load in loads[5:]:
        load.wait()
    fct[...] = dot(
        jnp.swapaxes(fcot[...], 0, 1).reshape(1152, 256), split_columns()[:, 128:384]
    ).astype(BF)

    def edge_wait(k, buf, row):
        for j in range(NC):
            pltpu.make_async_remote_copy(
                src_ref=z.at[pl.ds(0, 16)], dst_ref=buf.at[j], send_sem=edge_s.at[k], recv_sem=edge_r.at[k, j],
                device_id=(r, c), device_id_type=MESH,
            ).wait_recv()
        for j in range(NC):
            slots[j, row : row + 16, :] = buf[j]

    gu = gd = None
    for part in range(2):
        for n, (_, _, device) in reversed(list(enumerate(back_c))):
            a2a(part, n, c, device[1], device).wait_recv()

        if part == 0:
            pl.when(is_first)(functools.partial(edge_wait, 0, top, 0))
        else:
            pl.when(is_last)(functools.partial(edge_wait, 1, bot, 160))

        place_part(slots, rr, part)
        for p in range(3 * part, 3 * part + 3):
            coarse_pair(wc, rr, fc, p)

        if part == 0:

            @pl.when(has_prev)
            def _():
                fine_down.wait_recv()
                spread_fine(hf[0:2], u, 0)

            @pl.when(jnp.logical_not(has_prev))
            def _():
                u[0:96, :] = jnp.zeros((96, 512), BF)

            @pl.when(has_next)
            def _():
                fine_up.wait_recv()
                spread_fine(hf[2:3], u, 26)

            @pl.when(jnp.logical_not(has_next))
            def _():
                u[26 * 48 : 27 * 48, :] = jnp.zeros((48, 512), BF)

            fine_before(tb, u, g, has_prev)
            fine_group(tb, u, g, 0)
            fine_group(tb, u, g, 7)

        for p in range(3 * part, 3 * part + 3):
            a, b = join_pair(up, dm, g, fc, fct, ccot, jf, jc, p)
            gu = a if gu is None else gu + a
            gd = b if gd is None else gd + b

    acc[...] = pack(gu, gd).astype(acc.dtype)

    def swap(stage, n, src, dst, device):
        return pltpu.make_async_remote_copy(
            src_ref=src, dst_ref=dst, send_sem=ar_s.at[stage, n], recv_sem=ar_r.at[stage, n],
            device_id=device, device_id_type=MESH,
        )

    scatter = [swap(0, n, acc.at[k], s1.at[n], device) for n, (_, k, device) in enumerate(ahead_b)]
    for copy in scatter:
        copy.start()

    stores = [pltpu.make_async_copy(jft, jf_o, out_sem.at[0]), pltpu.make_async_copy(jc, jc_o, out_sem.at[1])]
    stores[1].start()
    jft[...] = jnp.swapaxes(dot(jf[...], join_columns()).astype(BF).reshape(24, 48, 256), 0, 1)
    stores[0].start()

    part = acc[beta].astype(F32)
    for n in reversed(range(NB - 1)):
        swap(0, n, acc.at[beta], s1.at[n], back_b[n][2]).wait_recv()
        part = part + s1[n].astype(F32)
    s2[alpha] = part.astype(s2.dtype)

    middle = [swap(1, n, s2.at[alpha], s2.at[alpha], device) for n, (_, _, device) in enumerate(ahead_a)]
    for copy in middle:
        copy.start()
    for n in reversed(range(NA - 1)):
        swap(1, n, s2.at[alpha], s2.at[back_a[n][0]], back_a[n][2]).wait_recv()
    part = s2[0].astype(F32)
    for k in range(1, NA):
        part = part + s2[k].astype(F32)
    s3[beta] = part.astype(s3.dtype)

    gather = [swap(2, n, s3.at[beta], s3.at[beta], device) for n, (_, _, device) in enumerate(ahead_b)]
    for copy in gather:
        copy.start()
    for n in reversed(range(NB - 1)):
        swap(2, n, s3.at[beta], s3.at[back_b[n][1]], back_b[n][2]).wait_recv()

    unpack(s3[...].astype(F32), gu_v, gd_v)
    grads = [pltpu.make_async_copy(gu_v, gu_o, out_sem.at[2]), pltpu.make_async_copy(gd_v, gd_o, out_sem.at[3])]
    for store in grads:
        store.start()

    @pl.when(has_below)
    def _():
        edge_down.wait_send()

    @pl.when(has_above)
    def _():
        edge_up.wait_send()

    @pl.when(has_next)
    def _():
        fine_down.wait_send()

    @pl.when(has_prev)
    def _():
        fine_up.wait_send()

    for copy in sends + scatter + middle + gather:
        copy.wait_send()
    for store in stores + grads:
        store.wait()


def write_out(*refs):
    sem = refs[8]
    copies = [pltpu.make_async_copy(refs[k], refs[4 + k], sem.at[k]) for k in range(4)]
    for copy in copies:
        copy.start()
    for copy in copies:
        copy.wait()


def shards(
    fine_in, coarse_in, fine_kernel, coarse_kernel, up_weight, down_weight, fine_cotangent, coarse_cotangent
):
    vmem, dma = pltpu.VMEM, pltpu.SemaphoreType.DMA
    anywhere = pl.BlockSpec(memory_space=pl.ANY)
    shapes = [((48, 24, 256), BF), ((12, 96, 128), BF), ((48, 96), F32), ((9, 48, 96), F32)]
    results = pl.pallas_call(
        kernel,
        out_shape=tuple(vmem(*shape) for shape in shapes),
        in_specs=[anywhere] * 8,
        out_specs=(anywhere,) * 4,
        scratch_shapes=[
            vmem((48, 24, 256), BF),
            vmem((12, 96, 128), BF),
            vmem((9, 48, 48), BF),
            vmem((9, 96, 96), BF),
            vmem((48, 96), BF),
            vmem((9, 48, 96), BF),
            vmem((48, 24, 256), BF),
            vmem((12, 96, 128), BF),
            dma((8,)),
            dma((4,)),
            vmem((3, 144, 240), BF),
            vmem((288, 384), BF),
            vmem((96, 432), BF),
            vmem((1184, 128), BF),
            vmem((24, 48, 256), BF),
            vmem((27 * 48, 512), BF),
            vmem((25 * 48, 384), BF),
            vmem((8, 176, 128), BF),
            vmem((14, 8, 16, 128), BF),
            vmem((6, 96, 256), BF),
            vmem((1152, 256), BF),
            vmem((1152, 256), BF),
            vmem((48, 24, 256), BF),
            vmem((12, 96, 128), BF),
            vmem((48, 96), F32),
            vmem((9, 48, 96), F32),
            vmem((8, 16, 128), BF),
            vmem((8, 16, 128), BF),
            vmem((3, 48, 256), BF),
            vmem((NB, 24, 128), BF),
            vmem((NB, 24, 128), BF),
            vmem((NA, 24, 128), BF),
            vmem((NB, 24, 128), BF),
            dma((2, NC)),
            dma((2, NC)),
            dma((2,)),
            dma((2, NC)),
            dma((2,)),
            dma((2,)),
            dma((3, 16)),
            dma((3, 16)),
        ],
        compiler_params=pltpu.CompilerParams(
            collective_id=0, has_side_effects=True, vmem_limit_bytes=40 << 20
        ),
    )(
        *[
            pltpu.with_memory_space_constraint(array, pltpu.HBM)
            for array in (
                fine_in,
                coarse_in,
                fine_kernel,
                coarse_kernel,
                up_weight,
                jnp.swapaxes(down_weight, 1, 2),
                fine_cotangent,
                jnp.swapaxes(coarse_cotangent, 0, 1),
            )
        ]
    )
    joined_fine, joined_coarse, grad_up, grad_down = pl.pallas_call(
        write_out,
        out_shape=tuple(pltpu.HBM(*shape) for shape in shapes),
        in_specs=[anywhere] * 4,
        out_specs=(anywhere,) * 4,
        scratch_shapes=[dma((4,))],
    )(*[pltpu.with_memory_space_constraint(array, pltpu.VMEM) for array in results])
    return joined_fine, jnp.swapaxes(joined_coarse, 0, 1), grad_up, jnp.swapaxes(grad_down, 1, 2)


def solution(mesh):
    strips = P(None, ("rows", "ch"), None)
    return jax.shard_map(
        shards,
        mesh=mesh,
        in_specs=(strips, P("ch", "rows", None), P(), P(), P(), P(), strips, strips),
        out_specs=(strips, strips, P(), P()),
        check_vma=False,
    )
```

```python
import functools

import jax
import jax.numpy as jnp
import numpy as np
from jax import lax
from jax.experimental import pallas as pl
from jax.experimental.pallas import tpu as pltpu
from jax.sharding import PartitionSpec as P

BF = jnp.bfloat16
F32 = jnp.float32
MESH = pl.DeviceIdType.MESH


def dot(a, b):
    return lax.dot_general(a, b, (((1,), (0,)), ((), ())), preferred_element_type=F32)


def dot_nt(a, b):
    return lax.dot_general(a, b, (((1,), (1,)), ((), ())), preferred_element_type=F32)


def one_hot(rows, cols, match):
    r = lax.broadcasted_iota(jnp.int32, (rows, cols), 0)
    c = lax.broadcasted_iota(jnp.int32, (rows, cols), 1)
    return jnp.where(match(r, c), 1.0, 0.0).astype(BF)


def split_columns():
    return one_hot(256, 512, lambda r, c: r == 2 * (c % 128) + c // 128 - 1)


def join_columns():
    return one_hot(256, 256, lambda r, c: c == 2 * (r % 128) + r // 128)


def gate(v):
    k, m = 0.7978845608028654, 0.044715
    q = v * v
    t = jnp.tanh(v * (k + (k * m) * q))
    half = 0.5 + 0.5 * t
    joined = v * half
    slope = half + (0.5 * v) * (1.0 - t * t) * (k + (3 * k * m) * q)
    return joined, slope


def prep_weights(fk, ck, dw, tb, wc, dm):
    fka = [fk[3 * a : 3 * a + 3].reshape(144, 48) for a in range(3)]
    for r in range(3):
        acc = None
        for a in range(3):
            d = dot(fka[a], one_hot(48, 240, lambda i, j: j == (r + a) * 48 + i))
            acc = d if acc is None else acc + d
        acc = acc.astype(BF)
        for b in range(3):
            tb[b, 48 * r : 48 * r + 48, :] = acc[48 * b : 48 * b + 48]
    place = one_hot(96, 128, lambda i, j: j == (i // 12) * 16 + i % 12)
    wide = dot(ck[...].reshape(864, 96), place).astype(BF)
    for t in range(9):
        a, b = t // 3, t % 3
        wc[96 * b : 96 * b + 96, 128 * a : 128 * a + 128] = wide[96 * t : 96 * t + 96]
    stacked = jnp.concatenate([dw[3 * a + b] for b in range(3) for a in range(3)], axis=0)
    dm[...] = stacked.T


def prep_coarse(ci, z):
    order = one_hot(192, 192, lambda r, k: k == (r % 12) * 16 + r // 12)
    for n in range(3):
        blocks = [ci[:, 16 * k : 16 * k + 16, :].reshape(192, 128) for k in (2 * n, 2 * n + 1)]
        out = dot(order, jnp.concatenate(blocks, axis=1)).astype(BF)
        for k in range(2):
            at = 16 + 192 * (2 * n + k)
            z[at : at + 192, :] = out[:, 128 * k : 128 * k + 128]
    z[0:16, :] = jnp.zeros((16, 128), BF)
    z[1168:1184, :] = jnp.zeros((16, 128), BF)


def place_part(slots, rr, part):
    (first, count), (row, rows) = PARTS[part], HEIGHTS[part]
    shift = 4 + 12 * row - first
    spread = one_hot(16 * rows, count, lambda r, k: (r % 16 < 12) & (k == shift + 12 * (r // 16) + r % 16))
    for n in range(4):
        both = [slots[k, first : first + count, :] for k in (2 * n, 2 * n + 1)]
        out = dot(spread, jnp.concatenate(both, axis=1)).astype(BF)
        for k in range(2):
            rr[row : row + rows, 2 * n + k] = out[:, 128 * k : 128 * k + 128].reshape(rows, 16, 128)


def spread_fine(rows, u, at):
    n = rows.shape[0]
    u[at * 48 : (at + n) * 48, :] = dot(rows.reshape(n * 48, 256), split_columns()).astype(BF)


def store_features(g, at, out):
    lane = lax.broadcasted_iota(jnp.int32, (48, 128), 1)
    shifted = jnp.where(lane == 0, 0.0, pltpu.roll(out[:, 128:], 1, 1))
    g[at * 48 : at * 48 + 48, :] = jnp.concatenate([shifted, out], axis=1).astype(BF)


def fine_group(tb, u, g, group):
    acc = None
    base = (3 * group + 1) * 48
    for b in range(3):
        d = dot(tb[b], u[base : base + 240, 128 * b : 128 * b + 256])
        acc = d if acc is None else acc + d
    for r in range(3):
        store_features(g, 3 * group + r + 1, acc[48 * r : 48 * r + 48])


def fine_before(tb, u, g, keep):
    acc = None
    for b in range(3):
        d = dot(tb[b, 0:48, 0:144], u[0:144, 128 * b : 128 * b + 256])
        acc = d if acc is None else acc + d
    store_features(g, 0, jnp.where(keep, acc, 0.0))


def coarse_pair(wc, rr, fc, p):
    i = 2 * p
    rows = jnp.concatenate(
        [rr[i : i + 3].reshape(384, 128), rr[i + 1 : i + 4].reshape(384, 128)], axis=1
    )
    y = dot(wc[...], rows)
    lane = lax.broadcasted_iota(jnp.int32, (96, 128), 1)
    for s in range(2):
        left = y[0:96, 128 * s : 128 * s + 128]
        mid = y[96:192, 128 * s : 128 * s + 128]
        right = y[192:288, 128 * s : 128 * s + 128]
        left = jnp.where(lane == 0, 0.0, pltpu.roll(left, 1, 1))
        right = jnp.where(lane == 127, 0.0, pltpu.roll(right, 127, 1))
        fc[p, :, 128 * s : 128 * s + 128] = (left + mid + right).astype(BF)


def windows(g, p):
    cols = []
    for i in (2 * p, 2 * p + 1):
        taps = [g[2 * i * 48 : (2 * i + 3) * 48, 128 * b : 128 * b + 128] for b in range(3)]
        cols.append(jnp.concatenate(taps, axis=0))
    return jnp.concatenate(cols, axis=1)


def join_pair(up, dm, g, fc, fcot, ccot, jf, jc, p):
    f = fc[p]
    lifted = dot(up[...], f)
    pooled = []
    for s in range(2):
        one = lifted[:, 128 * s : 128 * s + 128]
        both = jnp.concatenate([one, one], axis=1)
        total = None
        for a in range(2):
            h = 2 * (2 * p + s) + a
            pre = g[(h + 1) * 48 : (h + 2) * 48, 128:384].astype(F32) + both
            joined, slope = gate(pre)
            jf[h * 48 : (h + 1) * 48, :] = joined.astype(BF)
            term = (fcot[h * 48 : (h + 1) * 48, :].astype(F32) * slope).astype(BF).astype(F32)
            total = term if total is None else total + term
        pooled.append(total[:, :128] + total[:, 128:])
    pooled = jnp.concatenate(pooled, axis=1).astype(BF)
    gu = dot_nt(pooled, f)
    w = windows(g, p)
    pre = f.astype(F32) + dot(dm[...], w)
    joined, slope = gate(pre)
    for s in range(2):
        jc[2 * p + s] = joined[:, 128 * s : 128 * s + 128].astype(BF)
    cc = jnp.concatenate([ccot[2 * p], ccot[2 * p + 1]], axis=1).astype(F32)
    gd = dot_nt(w, (cc * slope).astype(BF))
    return gu, gd


def pack(gu, gd):
    rows = jnp.concatenate([gd, gu], axis=0)
    wide = jnp.concatenate([rows, jnp.zeros((480, 32), F32)], axis=1)
    tail = wide[384:480]
    lane = lax.broadcasted_iota(jnp.int32, (96, 128), 1)
    parts = []
    for k in range(4):
        head = wide[96 * k : 96 * k + 96]
        if k < 3:
            head = jnp.where(lane < 96, head, pltpu.roll(tail, 96 - 32 * k, 1))
        parts.append(head)
    return jnp.concatenate(parts, axis=0).reshape(16, 24, 128)


def unpack(total, grad_up, grad_down):
    flat = total.reshape(384, 128)
    lane = lax.broadcasted_iota(jnp.int32, (96, 128), 1)
    tail = None
    for k in range(3):
        moved = pltpu.roll(flat[96 * k : 96 * k + 96], (32 + 32 * k) % 128, 1)
        tail = moved if tail is None else jnp.where(lane < 32 * k, tail, moved)
    rows = jnp.concatenate([flat, tail], axis=0)[:, :96]
    for b in range(3):
        for a in range(3):
            k = 3 * b + a
            grad_down[3 * a + b] = rows[48 * k : 48 * k + 48]
    grad_up[...] = rows[432:480]


def farthest_first(sizes):
    def hops(digits):
        total = 0
        for name, step in zip(sizes, digits):
            if name == "core":
                total += 0.1 * step
            elif name == "x_hi":
                total += 2 * step
            elif name == "x_lo":
                total += step
            else:
                total += min(step, sizes[name] - step)
        return total

    every = [digits for digits in np.ndindex(*sizes.values()) if any(digits)]
    return sorted(every, key=lambda digits: -hops(digits))


SIZES = {"x_hi": 2, "z": 8, "core": 2, "y": 4, "x_lo": 2}
GROUP_A = {name: SIZES[name] for name in ("z", "core")}
GROUP_B = {name: SIZES[name] for name in ("x_hi", "y", "x_lo")}
GROUP_C = {name: SIZES[name] for name in ("y", "x_lo")}
ORDER_A, ORDER_B, ORDER_C = [farthest_first(group) for group in (GROUP_A, GROUP_B, GROUP_C)]
NR, NC, NA, NB = 32, 8, 16, 16
PARTS = ((0, 112), (112, 64))
HEIGHTS = ((0, 9), (9, 5))


def kernel(
    x_h, ci_h, fk_h, ck_h, up_h, dw_h, fcot_h, ccot_h,
    jf_o, jc_o, gu_o, gd_o,
    x, ci, fk, ck, up, dw, fcot, ccot, in_sem, out_sem,
    tb, wc, dm, z, t, u, g, slots, rr, fc, fct, jf, jft, jc,
    top, bot, hf, acc, s1, s2, s3,
    relay, a2a_s, a2a_r, edge_s, edge_r, fine_s, fine_r, ar_s, ar_r,
):
    loads = [
        pltpu.make_async_copy(src, dst, in_sem.at[k])
        for k, (src, dst) in enumerate(
            [(ci_h, ci), (x_h, x), (fk_h, fk), (ck_h, ck), (dw_h, dw), (up_h, up), (fcot_h, fcot), (ccot_h, ccot)]
        )
    ]
    for load in loads:
        load.start()

    r = lax.axis_index("rows")
    c = lax.axis_index("ch")
    alpha = lax.rem(r, NA)
    x_hi = r // NA
    beta = x_hi * NC + c
    here = {"x_hi": x_hi, "z": alpha // 2, "core": lax.rem(r, 2), "y": c // 2, "x_lo": lax.rem(c, 2)}

    def member(group, digits, sign):
        at = dict(here)
        for name, step in zip(group, digits):
            if step:
                step = step if sign > 0 else SIZES[name] - step
                at[name] = lax.rem(at[name] + step, SIZES[name])
        a = at["z"] * 2 + at["core"]
        ch = at["y"] * 2 + at["x_lo"]
        return a, at["x_hi"] * NC + ch, (at["x_hi"] * NA + a, ch)

    ahead_a = [member(GROUP_A, digits, 1) for digits in ORDER_A]
    ahead_b = [member(GROUP_B, digits, 1) for digits in ORDER_B]
    ahead_c = [member(GROUP_C, digits, 1) for digits in ORDER_C]
    back_a = [member(GROUP_A, digits, -1) for digits in ORDER_A]
    back_b = [member(GROUP_B, digits, -1) for digits in ORDER_B]
    back_c = [member(GROUP_C, digits, -1) for digits in ORDER_C]

    barrier = pltpu.get_barrier_semaphore()

    def greet(device):
        pl.semaphore_signal(barrier, inc=1, device_id=device, device_id_type=MESH)

    first_row, last_row = r == 0, r == NR - 1
    has_above, has_below = jnp.logical_not(first_row), jnp.logical_not(last_row)
    is_first = jnp.logical_and(c == 0, has_above)
    is_last = jnp.logical_and(c == NC - 1, has_below)

    for _, _, device in ahead_b:
        greet(device)

    @pl.when(has_below)
    def _():
        greet((r + 1, 0))

    @pl.when(has_above)
    def _():
        greet((r - 1, NC - 1))

    @pl.when(is_first)
    def _():
        for k in range(NC):
            greet((r - 1, k))

    @pl.when(is_last)
    def _():
        for k in range(NC):
            greet((r + 1, k))

    def along_z(step, flip):
        core = lax.rem(here["core"] + flip, 2)
        return (x_hi * NA + lax.rem(here["z"] + step + 8, 8) * 2 + core, c)

    for step, flip in ((0, 1), (1, 0), (-1, 0), (1, 1), (-1, 1)):
        greet(along_z(step, flip))

    loads[0].wait()
    prep_coarse(ci, z)

    one = jnp.int32(1)
    zero = jnp.int32(0)
    peers = NB - 1 + 5
    peers = peers + jnp.where(has_below, one, zero) + jnp.where(has_above, one, zero)
    peers = peers + jnp.where(is_first, NC * one, zero) + jnp.where(is_last, NC * one, zero)
    pl.semaphore_wait(barrier, peers)

    def pass_on(stage, step):
        pl.semaphore_signal(relay.at[stage], inc=1, device_id=along_z(step, 0), device_id_type=MESH)

    pass_on(0, 1)
    pass_on(0, -1)

    def a2a(part, n, row, slot, device):
        first, count = PARTS[part]
        return pltpu.make_async_remote_copy(
            src_ref=z.at[pl.ds(pl.multiple_of(144 * row + first, 16), count)],
            dst_ref=slots.at[slot, pl.ds(first, count)],
            send_sem=a2a_s.at[part, n],
            recv_sem=a2a_r.at[part, n],
            device_id=device,
            device_id_type=MESH,
        )

    sends = [
        a2a(part, n, device[1], c, device) for part in range(2) for n, (_, _, device) in enumerate(ahead_c)
    ]
    for copy in sends[:7]:
        copy.start()

    def edge(k, src, dst, device):
        return pltpu.make_async_remote_copy(
            src_ref=src, dst_ref=dst, send_sem=edge_s.at[k], recv_sem=edge_r.at[k, c],
            device_id=device, device_id_type=MESH,
        )

    edge_down = edge(0, z.at[pl.ds(1152, 16)], top.at[c], (r + 1, 0))
    edge_up = edge(1, z.at[pl.ds(16, 16)], bot.at[c], (r - 1, NC - 1))

    @pl.when(has_below)
    def _():
        edge_down.start()

    @pl.when(has_above)
    def _():
        edge_up.start()

    wraps_down = c == NC - 1
    wraps_up = c == 0
    has_next = jnp.logical_not(jnp.logical_and(wraps_down, last_row))
    has_prev = jnp.logical_not(jnp.logical_and(wraps_up, first_row))
    next_dev = (r + jnp.where(wraps_down, one, zero), lax.rem(c + 1, NC))
    prev_dev = (r - jnp.where(wraps_up, one, zero), lax.rem(c + NC - 1, NC))

    def halo(k, src, dst, device):
        return pltpu.make_async_remote_copy(
            src_ref=src, dst_ref=dst, send_sem=fine_s.at[k], recv_sem=fine_r.at[k],
            device_id=device, device_id_type=MESH,
        )

    loads[1].wait()
    t[...] = jnp.swapaxes(x[...], 0, 1)
    fine_down = halo(0, t.at[pl.ds(22, 2)], hf.at[pl.ds(0, 2)], next_dev)
    fine_up = halo(1, t.at[pl.ds(0, 1)], hf.at[pl.ds(2, 1)], prev_dev)

    @pl.when(has_next)
    def _():
        fine_down.start()

    @pl.when(has_prev)
    def _():
        fine_up.start()

    for copy in sends[7:]:
        copy.start()
    slots[pl.ds(c, 1)] = z[pl.ds(pl.multiple_of(144 * c, 16), 176), :].reshape(1, 176, 128)

    for load in loads[2:5]:
        load.wait()
    prep_weights(fk, ck, dw, tb, wc, dm)
    spread_fine(t[...], u, 2)
    for k in range(1, 7):
        fine_group(tb, u, g, k)
    pl.semaphore_wait(relay.at[0], 2)
    pass_on(1, 2)
    pass_on(1, -2)
    for load in loads[5:]:
        load.wait()
    fct[...] = dot(
        jnp.swapaxes(fcot[...], 0, 1).reshape(1152, 256), split_columns()[:, 128:384]
    ).astype(BF)

    def edge_wait(k, buf, row):
        for j in range(NC):
            pltpu.make_async_remote_copy(
                src_ref=z.at[pl.ds(0, 16)], dst_ref=buf.at[j], send_sem=edge_s.at[k], recv_sem=edge_r.at[k, j],
                device_id=(r, c), device_id_type=MESH,
            ).wait_recv()
        for j in range(NC):
            slots[j, row : row + 16, :] = buf[j]

    gu = gd = None
    for part in range(2):
        for n, (_, _, device) in reversed(list(enumerate(back_c))):
            a2a(part, n, c, device[1], device).wait_recv()

        if part == 0:
            pl.when(is_first)(functools.partial(edge_wait, 0, top, 0))
        else:
            pl.when(is_last)(functools.partial(edge_wait, 1, bot, 160))

        place_part(slots, rr, part)
        for p in range(3 * part, 3 * part + 3):
            coarse_pair(wc, rr, fc, p)

        if part == 0:

            @pl.when(has_prev)
            def _():
                fine_down.wait_recv()
                spread_fine(hf[0:2], u, 0)

            @pl.when(jnp.logical_not(has_prev))
            def _():
                u[0:96, :] = jnp.zeros((96, 512), BF)

            @pl.when(has_next)
            def _():
                fine_up.wait_recv()
                spread_fine(hf[2:3], u, 26)

            @pl.when(jnp.logical_not(has_next))
            def _():
                u[26 * 48 : 27 * 48, :] = jnp.zeros((48, 512), BF)

            fine_before(tb, u, g, has_prev)
            fine_group(tb, u, g, 0)
            fine_group(tb, u, g, 7)

        for p in range(3 * part, 3 * part + 3):
            a, b = join_pair(up, dm, g, fc, fct, ccot, jf, jc, p)
            gu = a if gu is None else gu + a
            gd = b if gd is None else gd + b

    acc[...] = pack(gu, gd).astype(acc.dtype)

    def swap(stage, n, src, dst, device):
        return pltpu.make_async_remote_copy(
            src_ref=src, dst_ref=dst, send_sem=ar_s.at[stage, n], recv_sem=ar_r.at[stage, n],
            device_id=device, device_id_type=MESH,
        )

    scatter = [swap(0, n, acc.at[k], s1.at[n], device) for n, (_, k, device) in enumerate(ahead_b)]
    for copy in scatter:
        copy.start()

    stores = [pltpu.make_async_copy(jft, jf_o, out_sem.at[0]), pltpu.make_async_copy(jc, jc_o, out_sem.at[1])]
    stores[1].start()
    jft[...] = jnp.swapaxes(dot(jf[...], join_columns()).astype(BF).reshape(24, 48, 256), 0, 1)
    stores[0].start()

    @pl.when(has_below)
    def _():
        edge_down.wait_send()

    @pl.when(has_above)
    def _():
        edge_up.wait_send()

    @pl.when(has_next)
    def _():
        fine_down.wait_send()

    @pl.when(has_prev)
    def _():
        fine_up.wait_send()

    for copy in sends:
        copy.wait_send()

    part = acc[beta].astype(F32)
    for n in reversed(range(NB - 1)):
        swap(0, n, acc.at[beta], s1.at[n], back_b[n][2]).wait_recv()
        part = part + s1[n].astype(F32)
    s2[alpha] = part.astype(s2.dtype)

    pl.semaphore_wait(relay.at[1], 2)
    middle = [swap(1, n, s2.at[alpha], s2.at[alpha], device) for n, (_, _, device) in enumerate(ahead_a)]
    for copy in middle:
        copy.start()
    for copy in scatter:
        copy.wait_send()
    for store in stores:
        store.wait()
    for n in reversed(range(NA - 1)):
        swap(1, n, s2.at[alpha], s2.at[back_a[n][0]], back_a[n][2]).wait_recv()
    part = s2[0].astype(F32)
    for k in range(1, NA):
        part = part + s2[k].astype(F32)
    s3[beta] = part.astype(s3.dtype)

    gather = [swap(2, n, s3.at[beta], s3.at[beta], device) for n, (_, _, device) in enumerate(ahead_b)]
    for copy in gather:
        copy.start()
    for copy in middle:
        copy.wait_send()
    for n in reversed(range(NB - 1)):
        swap(2, n, s3.at[beta], s3.at[back_b[n][1]], back_b[n][2]).wait_recv()

    unpack(s3[...].astype(F32), gu_o, gd_o)
    for copy in gather:
        copy.wait_send()


def write_out(*refs):
    sem = refs[8]
    copies = [pltpu.make_async_copy(refs[k], refs[4 + k], sem.at[k]) for k in range(4)]
    for copy in copies:
        copy.start()
    for copy in copies:
        copy.wait()


def shards(
    fine_in, coarse_in, fine_kernel, coarse_kernel, up_weight, down_weight, fine_cotangent, coarse_cotangent
):
    vmem, dma = pltpu.VMEM, pltpu.SemaphoreType.DMA
    anywhere = pl.BlockSpec(memory_space=pl.ANY)
    shapes = [((48, 24, 256), BF), ((12, 96, 128), BF), ((48, 96), F32), ((9, 48, 96), F32)]
    results = pl.pallas_call(
        kernel,
        out_shape=tuple(vmem(*shape) for shape in shapes),
        in_specs=[anywhere] * 8,
        out_specs=(anywhere,) * 2 + (pl.BlockSpec(memory_space=pltpu.VMEM),) * 2,
        scratch_shapes=[
            vmem((48, 24, 256), BF),
            vmem((12, 96, 128), BF),
            vmem((9, 48, 48), BF),
            vmem((9, 96, 96), BF),
            vmem((48, 96), BF),
            vmem((9, 48, 96), BF),
            vmem((48, 24, 256), BF),
            vmem((12, 96, 128), BF),
            dma((8,)),
            dma((4,)),
            vmem((3, 144, 240), BF),
            vmem((288, 384), BF),
            vmem((96, 432), BF),
            vmem((1184, 128), BF),
            vmem((24, 48, 256), BF),
            vmem((27 * 48, 512), BF),
            vmem((25 * 48, 384), BF),
            vmem((8, 176, 128), BF),
            vmem((14, 8, 16, 128), BF),
            vmem((6, 96, 256), BF),
            vmem((1152, 256), BF),
            vmem((1152, 256), BF),
            vmem((48, 24, 256), BF),
            vmem((12, 96, 128), BF),
            vmem((8, 16, 128), BF),
            vmem((8, 16, 128), BF),
            vmem((3, 48, 256), BF),
            vmem((NB, 24, 128), BF),
            vmem((NB, 24, 128), BF),
            vmem((NA, 24, 128), BF),
            vmem((NB, 24, 128), BF),
            pltpu.SemaphoreType.REGULAR((2,)),
            dma((2, NC)),
            dma((2, NC)),
            dma((2,)),
            dma((2, NC)),
            dma((2,)),
            dma((2,)),
            dma((3, 16)),
            dma((3, 16)),
        ],
        compiler_params=pltpu.CompilerParams(
            collective_id=0, has_side_effects=True, vmem_limit_bytes=40 << 20
        ),
    )(
        *[
            pltpu.with_memory_space_constraint(array, pltpu.HBM)
            for array in (
                fine_in,
                coarse_in,
                fine_kernel,
                coarse_kernel,
                up_weight,
                jnp.swapaxes(down_weight, 1, 2),
                fine_cotangent,
                jnp.swapaxes(coarse_cotangent, 0, 1),
            )
        ]
    )
    joined_fine, joined_coarse, grad_up, grad_down = pl.pallas_call(
        write_out,
        out_shape=tuple(pltpu.HBM(*shape) for shape in shapes),
        in_specs=[anywhere] * 4,
        out_specs=(anywhere,) * 4,
        scratch_shapes=[dma((4,))],
    )(*[pltpu.with_memory_space_constraint(array, pltpu.VMEM) for array in results])
    return joined_fine, jnp.swapaxes(joined_coarse, 0, 1), grad_up, jnp.swapaxes(grad_down, 1, 2)


def solution(mesh):
    strips = P(None, ("rows", "ch"), None)
    return jax.shard_map(
        shards,
        mesh=mesh,
        in_specs=(strips, P("ch", "rows", None), P(), P(), P(), P(), strips, strips),
        out_specs=(strips, strips, P(), P()),
        check_vma=False,
    )
```

```python
import functools

import jax
import jax.numpy as jnp
import numpy as np
from jax import lax
from jax.experimental import pallas as pl
from jax.experimental.pallas import tpu as pltpu
from jax.sharding import PartitionSpec as P

BF = jnp.bfloat16
F32 = jnp.float32
MESH = pl.DeviceIdType.MESH


def dot(a, b):
    return lax.dot_general(a, b, (((1,), (0,)), ((), ())), preferred_element_type=F32)


def dot_nt(a, b):
    return lax.dot_general(a, b, (((1,), (1,)), ((), ())), preferred_element_type=F32)


def one_hot(rows, cols, match):
    r = lax.broadcasted_iota(jnp.int32, (rows, cols), 0)
    c = lax.broadcasted_iota(jnp.int32, (rows, cols), 1)
    return jnp.where(match(r, c), 1.0, 0.0).astype(BF)


def split_columns():
    return one_hot(256, 512, lambda r, c: r == 2 * (c % 128) + c // 128 - 1)


def join_columns():
    return one_hot(256, 256, lambda r, c: c == 2 * (r % 128) + r // 128)


def gate(v):
    k, m = 0.7978845608028654, 0.044715
    q = v * v
    h = 0.5 * jnp.tanh(v * (k + (k * m) * q))
    half = 0.5 + h
    joined = v * half
    slope = half + joined * (0.5 - h) * (2 * k + (6 * k * m) * q)
    return joined, slope


def prep_weights(fk, ck, dw, tb, wc, dm):
    fka = [fk[3 * a : 3 * a + 3].reshape(144, 48) for a in range(3)]
    for r in range(3):
        acc = None
        for a in range(3):
            d = dot(fka[a], one_hot(48, 240, lambda i, j: j == (r + a) * 48 + i))
            acc = d if acc is None else acc + d
        acc = acc.astype(BF)
        for b in range(3):
            tb[b, 48 * r : 48 * r + 48, :] = acc[48 * b : 48 * b + 48]
    place = one_hot(96, 128, lambda i, j: j == (i // 12) * 16 + i % 12)
    wide = dot(ck[...].reshape(864, 96), place).astype(BF)
    for t in range(9):
        a, b = t // 3, t % 3
        wc[96 * b : 96 * b + 96, 128 * a : 128 * a + 128] = wide[96 * t : 96 * t + 96]
    stacked = jnp.concatenate([dw[3 * a + b] for b in range(3) for a in range(3)], axis=0)
    dm[...] = stacked.T


def prep_coarse(ci, z):
    order = one_hot(192, 192, lambda r, k: k == (r % 12) * 16 + r // 12)
    for n in range(3):
        blocks = [ci[:, 16 * k : 16 * k + 16, :].reshape(192, 128) for k in (2 * n, 2 * n + 1)]
        out = dot(order, jnp.concatenate(blocks, axis=1)).astype(BF)
        for k in range(2):
            at = 16 + 192 * (2 * n + k)
            z[at : at + 192, :] = out[:, 128 * k : 128 * k + 128]
    z[0:16, :] = jnp.zeros((16, 128), BF)
    z[1168:1184, :] = jnp.zeros((16, 128), BF)


def place_part(slots, rr, part):
    (first, count), (row, rows) = PARTS[part], HEIGHTS[part]
    shift = 4 + 12 * row - first
    spread = one_hot(16 * rows, count, lambda r, k: (r % 16 < 12) & (k == shift + 12 * (r // 16) + r % 16))
    for n in range(4):
        both = [slots[k, first : first + count, :] for k in (2 * n, 2 * n + 1)]
        out = dot(spread, jnp.concatenate(both, axis=1)).astype(BF)
        for k in range(2):
            rr[row : row + rows, 2 * n + k] = out[:, 128 * k : 128 * k + 128].reshape(rows, 16, 128)


def spread_fine(rows, u, at):
    n = rows.shape[0]
    u[at * 48 : (at + n) * 48, :] = dot(rows.reshape(n * 48, 256), split_columns()).astype(BF)


def store_features(g, at, out):
    lane = lax.broadcasted_iota(jnp.int32, (48, 128), 1)
    shifted = jnp.where(lane == 0, 0.0, pltpu.roll(out[:, 128:], 1, 1))
    g[at * 48 : at * 48 + 48, :] = jnp.concatenate([shifted, out], axis=1).astype(BF)


def fine_group(tb, u, g, group):
    acc = None
    base = (3 * group + 1) * 48
    for b in range(3):
        d = dot(tb[b], u[base : base + 240, 128 * b : 128 * b + 256])
        acc = d if acc is None else acc + d
    for r in range(3):
        store_features(g, 3 * group + r + 1, acc[48 * r : 48 * r + 48])


def fine_before(tb, u, g, keep):
    acc = None
    for b in range(3):
        d = dot(tb[b, 0:48, 0:144], u[0:144, 128 * b : 128 * b + 256])
        acc = d if acc is None else acc + d
    store_features(g, 0, jnp.where(keep, acc, 0.0))


def coarse_pair(wc, rr, fc, p):
    i = 2 * p
    rows = jnp.concatenate(
        [rr[i : i + 3].reshape(384, 128), rr[i + 1 : i + 4].reshape(384, 128)], axis=1
    )
    y = dot(wc[...], rows)
    lane = lax.broadcasted_iota(jnp.int32, (96, 128), 1)
    for s in range(2):
        left = y[0:96, 128 * s : 128 * s + 128]
        mid = y[96:192, 128 * s : 128 * s + 128]
        right = y[192:288, 128 * s : 128 * s + 128]
        left = jnp.where(lane == 0, 0.0, pltpu.roll(left, 1, 1))
        right = jnp.where(lane == 127, 0.0, pltpu.roll(right, 127, 1))
        fc[p, :, 128 * s : 128 * s + 128] = (left + mid + right).astype(BF)


def windows(g, p):
    cols = []
    for i in (2 * p, 2 * p + 1):
        taps = [g[2 * i * 48 : (2 * i + 3) * 48, 128 * b : 128 * b + 128] for b in range(3)]
        cols.append(jnp.concatenate(taps, axis=0))
    return jnp.concatenate(cols, axis=1)


def join_pair(up, dm, g, fc, fcot, ccot, jf, jc, p):
    f = fc[p]
    lifted = dot(up[...], f)
    pooled = []
    for s in range(2):
        one = lifted[:, 128 * s : 128 * s + 128]
        both = jnp.concatenate([one, one], axis=1)
        total = None
        for a in range(2):
            h = 2 * (2 * p + s) + a
            pre = g[(h + 1) * 48 : (h + 2) * 48, 128:384].astype(F32) + both
            joined, slope = gate(pre)
            jf[h * 48 : (h + 1) * 48, :] = joined.astype(BF)
            term = (fcot[h * 48 : (h + 1) * 48, :].astype(F32) * slope).astype(BF).astype(F32)
            total = term if total is None else total + term
        pooled.append(total[:, :128] + total[:, 128:])
    pooled = jnp.concatenate(pooled, axis=1).astype(BF)
    w = windows(g, p)
    pre = f.astype(F32) + dot(dm[...], w)
    joined, slope = gate(pre)
    for s in range(2):
        jc[2 * p + s] = joined[:, 128 * s : 128 * s + 128].astype(BF)
    cc = jnp.concatenate([ccot[2 * p], ccot[2 * p + 1]], axis=1).astype(F32)
    return pooled, f, (cc * slope).astype(BF), w


def pack(gu, gd):
    rows = jnp.concatenate([gd, gu], axis=0)
    wide = jnp.concatenate([rows, jnp.zeros((480, 32), F32)], axis=1)
    tail = wide[384:480]
    lane = lax.broadcasted_iota(jnp.int32, (96, 128), 1)
    parts = []
    for k in range(4):
        head = wide[96 * k : 96 * k + 96]
        if k < 3:
            head = jnp.where(lane < 96, head, pltpu.roll(tail, 96 - 32 * k, 1))
        parts.append(head)
    return jnp.concatenate(parts, axis=0).reshape(16, 24, 128)


def unpack(total, grad_up, grad_down):
    flat = total.reshape(384, 128)
    lane = lax.broadcasted_iota(jnp.int32, (96, 128), 1)
    tail = None
    for k in range(3):
        moved = pltpu.roll(flat[96 * k : 96 * k + 96], (32 + 32 * k) % 128, 1)
        tail = moved if tail is None else jnp.where(lane < 32 * k, tail, moved)
    rows = jnp.concatenate([flat, tail], axis=0)[:, :96]
    for b in range(3):
        for a in range(3):
            k = 3 * b + a
            grad_down[3 * a + b] = rows[48 * k : 48 * k + 48]
    grad_up[...] = rows[432:480]


def farthest_first(sizes):
    def hops(digits):
        total = 0
        for name, step in zip(sizes, digits):
            if name == "core":
                total += 0.1 * step
            elif name == "x_hi":
                total += 2 * step
            elif name == "x_lo":
                total += step
            else:
                total += min(step, sizes[name] - step)
        return total

    every = [digits for digits in np.ndindex(*sizes.values()) if any(digits)]
    return sorted(every, key=lambda digits: -hops(digits))


SIZES = {"x_hi": 2, "z": 8, "core": 2, "y": 4, "x_lo": 2}
GROUP_A = {name: SIZES[name] for name in ("z", "core")}
GROUP_B = {name: SIZES[name] for name in ("x_hi", "y", "x_lo")}
GROUP_C = {name: SIZES[name] for name in ("y", "x_lo")}
ORDER_A, ORDER_B, ORDER_C = [farthest_first(group) for group in (GROUP_A, GROUP_B, GROUP_C)]
NR, NC, NA, NB = 32, 8, 16, 16
PARTS = ((0, 112), (112, 64))
HEIGHTS = ((0, 9), (9, 5))


def kernel(
    x_h, ci_h, fk_h, ck_h, up_h, dw_h, fcot_h, ccot_h,
    jf_o, jc_o, gu_o, gd_o,
    x, ci, fk, ck, up, dw, fcot, ccot, in_sem, out_sem,
    tb, wc, dm, z, t, u, g, slots, rr, fc, fct, jf, jft, jc,
    top, bot, hf, acc, s1, s2, s3,
    relay, a2a_s, a2a_r, edge_s, edge_r, fine_s, fine_r, ar_s, ar_r,
):
    loads = [
        pltpu.make_async_copy(src, dst, in_sem.at[k])
        for k, (src, dst) in enumerate(
            [(ci_h, ci), (x_h, x), (fk_h, fk), (ck_h, ck), (dw_h, dw), (up_h, up), (fcot_h, fcot), (ccot_h, ccot)]
        )
    ]
    for load in loads:
        load.start()

    r = lax.axis_index("rows")
    c = lax.axis_index("ch")
    alpha = lax.rem(r, NA)
    x_hi = r // NA
    beta = x_hi * NC + c
    here = {"x_hi": x_hi, "z": alpha // 2, "core": lax.rem(r, 2), "y": c // 2, "x_lo": lax.rem(c, 2)}

    def member(group, digits, sign):
        at = dict(here)
        for name, step in zip(group, digits):
            if step:
                step = step if sign > 0 else SIZES[name] - step
                at[name] = lax.rem(at[name] + step, SIZES[name])
        a = at["z"] * 2 + at["core"]
        ch = at["y"] * 2 + at["x_lo"]
        return a, at["x_hi"] * NC + ch, (at["x_hi"] * NA + a, ch)

    ahead_a = [member(GROUP_A, digits, 1) for digits in ORDER_A]
    ahead_b = [member(GROUP_B, digits, 1) for digits in ORDER_B]
    ahead_c = [member(GROUP_C, digits, 1) for digits in ORDER_C]
    back_a = [member(GROUP_A, digits, -1) for digits in ORDER_A]
    back_b = [member(GROUP_B, digits, -1) for digits in ORDER_B]
    back_c = [member(GROUP_C, digits, -1) for digits in ORDER_C]

    barrier = pltpu.get_barrier_semaphore()

    def greet(device):
        pl.semaphore_signal(barrier, inc=1, device_id=device, device_id_type=MESH)

    first_row, last_row = r == 0, r == NR - 1
    has_above, has_below = jnp.logical_not(first_row), jnp.logical_not(last_row)
    is_first = jnp.logical_and(c == 0, has_above)
    is_last = jnp.logical_and(c == NC - 1, has_below)

    for _, _, device in ahead_b:
        greet(device)

    @pl.when(has_below)
    def _():
        greet((r + 1, 0))

    @pl.when(has_above)
    def _():
        greet((r - 1, NC - 1))

    @pl.when(is_first)
    def _():
        for k in range(NC):
            greet((r - 1, k))

    @pl.when(is_last)
    def _():
        for k in range(NC):
            greet((r + 1, k))

    def along_z(step, flip):
        core = lax.rem(here["core"] + flip, 2)
        return (x_hi * NA + lax.rem(here["z"] + step + 8, 8) * 2 + core, c)

    for step, flip in ((0, 1), (1, 0), (-1, 0), (1, 1), (-1, 1)):
        greet(along_z(step, flip))

    loads[0].wait()
    prep_coarse(ci, z)

    one = jnp.int32(1)
    zero = jnp.int32(0)
    peers = NB - 1 + 5
    peers = peers + jnp.where(has_below, one, zero) + jnp.where(has_above, one, zero)
    peers = peers + jnp.where(is_first, NC * one, zero) + jnp.where(is_last, NC * one, zero)
    pl.semaphore_wait(barrier, peers)

    def pass_on(stage, step):
        pl.semaphore_signal(relay.at[stage], inc=1, device_id=along_z(step, 0), device_id_type=MESH)

    pass_on(0, 1)
    pass_on(0, -1)

    def a2a(part, n, row, slot, device):
        first, count = PARTS[part]
        return pltpu.make_async_remote_copy(
            src_ref=z.at[pl.ds(pl.multiple_of(144 * row + first, 16), count)],
            dst_ref=slots.at[slot, pl.ds(first, count)],
            send_sem=a2a_s.at[part, n],
            recv_sem=a2a_r.at[part, n],
            device_id=device,
            device_id_type=MESH,
        )

    sends = [
        a2a(part, n, device[1], c, device) for part in range(2) for n, (_, _, device) in enumerate(ahead_c)
    ]
    for copy in sends[:7]:
        copy.start()

    def edge(k, src, dst, device):
        return pltpu.make_async_remote_copy(
            src_ref=src, dst_ref=dst, send_sem=edge_s.at[k], recv_sem=edge_r.at[k, c],
            device_id=device, device_id_type=MESH,
        )

    edge_down = edge(0, z.at[pl.ds(1152, 16)], top.at[c], (r + 1, 0))
    edge_up = edge(1, z.at[pl.ds(16, 16)], bot.at[c], (r - 1, NC - 1))

    @pl.when(has_below)
    def _():
        edge_down.start()

    @pl.when(has_above)
    def _():
        edge_up.start()

    wraps_down = c == NC - 1
    wraps_up = c == 0
    has_next = jnp.logical_not(jnp.logical_and(wraps_down, last_row))
    has_prev = jnp.logical_not(jnp.logical_and(wraps_up, first_row))
    next_dev = (r + jnp.where(wraps_down, one, zero), lax.rem(c + 1, NC))
    prev_dev = (r - jnp.where(wraps_up, one, zero), lax.rem(c + NC - 1, NC))

    def halo(k, src, dst, device):
        return pltpu.make_async_remote_copy(
            src_ref=src, dst_ref=dst, send_sem=fine_s.at[k], recv_sem=fine_r.at[k],
            device_id=device, device_id_type=MESH,
        )

    loads[1].wait()
    t[...] = jnp.swapaxes(x[...], 0, 1)
    fine_down = halo(0, t.at[pl.ds(22, 2)], hf.at[pl.ds(0, 2)], next_dev)
    fine_up = halo(1, t.at[pl.ds(0, 1)], hf.at[pl.ds(2, 1)], prev_dev)

    @pl.when(has_next)
    def _():
        fine_down.start()

    @pl.when(has_prev)
    def _():
        fine_up.start()

    for copy in sends[7:]:
        copy.start()
    slots[pl.ds(c, 1)] = z[pl.ds(pl.multiple_of(144 * c, 16), 176), :].reshape(1, 176, 128)

    for load in loads[2:5]:
        load.wait()
    prep_weights(fk, ck, dw, tb, wc, dm)
    spread_fine(t[...], u, 2)
    for k in range(1, 7):
        fine_group(tb, u, g, k)
    pl.semaphore_wait(relay.at[0], 2)
    pass_on(1, 2)
    pass_on(1, -2)
    for load in loads[5:]:
        load.wait()
    fct[...] = dot(
        jnp.swapaxes(fcot[...], 0, 1).reshape(1152, 256), split_columns()[:, 128:384]
    ).astype(BF)

    def edge_wait(k, buf, row):
        for j in range(NC):
            pltpu.make_async_remote_copy(
                src_ref=z.at[pl.ds(0, 16)], dst_ref=buf.at[j], send_sem=edge_s.at[k], recv_sem=edge_r.at[k, j],
                device_id=(r, c), device_id_type=MESH,
            ).wait_recv()
        for j in range(NC):
            slots[j, row : row + 16, :] = buf[j]

    gu = gd = None
    for part in range(2):
        for n, (_, _, device) in reversed(list(enumerate(back_c))):
            a2a(part, n, c, device[1], device).wait_recv()

        if part == 0:
            pl.when(is_first)(functools.partial(edge_wait, 0, top, 0))
        else:
            pl.when(is_last)(functools.partial(edge_wait, 1, bot, 160))

        place_part(slots, rr, part)
        for p in range(3 * part, 3 * part + 3):
            coarse_pair(wc, rr, fc, p)

        if part == 0:

            @pl.when(has_prev)
            def _():
                fine_down.wait_recv()
                spread_fine(hf[0:2], u, 0)

            @pl.when(jnp.logical_not(has_prev))
            def _():
                u[0:96, :] = jnp.zeros((96, 512), BF)

            @pl.when(has_next)
            def _():
                fine_up.wait_recv()
                spread_fine(hf[2:3], u, 26)

            @pl.when(jnp.logical_not(has_next))
            def _():
                u[26 * 48 : 27 * 48, :] = jnp.zeros((48, 512), BF)

            fine_before(tb, u, g, has_prev)
            fine_group(tb, u, g, 0)
            fine_group(tb, u, g, 7)

        terms = [
            join_pair(up, dm, g, fc, fct, ccot, jf, jc, p) for p in range(3 * part, 3 * part + 3)
        ]
        pooled, f, slope, taps = [jnp.concatenate(term, axis=1) for term in zip(*terms)]
        a, b = dot_nt(pooled, f), dot_nt(taps, slope)
        gu = a if gu is None else gu + a
        gd = b if gd is None else gd + b

    acc[...] = pack(gu, gd).astype(acc.dtype)

    def swap(stage, n, src, dst, device):
        return pltpu.make_async_remote_copy(
            src_ref=src, dst_ref=dst, send_sem=ar_s.at[stage, n], recv_sem=ar_r.at[stage, n],
            device_id=device, device_id_type=MESH,
        )

    scatter = [swap(0, n, acc.at[k], s1.at[n], device) for n, (_, k, device) in enumerate(ahead_b)]
    for copy in scatter:
        copy.start()

    stores = [pltpu.make_async_copy(jft, jf_o, out_sem.at[0]), pltpu.make_async_copy(jc, jc_o, out_sem.at[1])]
    stores[1].start()
    jft[...] = jnp.swapaxes(dot(jf[...], join_columns()).astype(BF).reshape(24, 48, 256), 0, 1)
    stores[0].start()

    @pl.when(has_below)
    def _():
        edge_down.wait_send()

    @pl.when(has_above)
    def _():
        edge_up.wait_send()

    @pl.when(has_next)
    def _():
        fine_down.wait_send()

    @pl.when(has_prev)
    def _():
        fine_up.wait_send()

    for copy in sends:
        copy.wait_send()

    part = acc[beta].astype(F32)
    for n in reversed(range(NB - 1)):
        swap(0, n, acc.at[beta], s1.at[n], back_b[n][2]).wait_recv()
        part = part + s1[n].astype(F32)
    s2[alpha] = part.astype(s2.dtype)

    pl.semaphore_wait(relay.at[1], 2)
    middle = [swap(1, n, s2.at[alpha], s2.at[alpha], device) for n, (_, _, device) in enumerate(ahead_a)]
    for copy in middle:
        copy.start()
    for copy in scatter:
        copy.wait_send()
    for store in stores:
        store.wait()
    for n in reversed(range(NA - 1)):
        swap(1, n, s2.at[alpha], s2.at[back_a[n][0]], back_a[n][2]).wait_recv()
    part = s2[0].astype(F32)
    for k in range(1, NA):
        part = part + s2[k].astype(F32)
    s3[beta] = part.astype(s3.dtype)

    gather = [swap(2, n, s3.at[beta], s3.at[beta], device) for n, (_, _, device) in enumerate(ahead_b)]
    for copy in gather:
        copy.start()
    for copy in middle:
        copy.wait_send()
    for n in reversed(range(NB - 1)):
        swap(2, n, s3.at[beta], s3.at[back_b[n][1]], back_b[n][2]).wait_recv()

    unpack(s3[...].astype(F32), gu_o, gd_o)
    for copy in gather:
        copy.wait_send()


def write_out(*refs):
    sem = refs[8]
    copies = [pltpu.make_async_copy(refs[k], refs[4 + k], sem.at[k]) for k in range(4)]
    for copy in copies:
        copy.start()
    for copy in copies:
        copy.wait()


def shards(
    fine_in, coarse_in, fine_kernel, coarse_kernel, up_weight, down_weight, fine_cotangent, coarse_cotangent
):
    vmem, dma = pltpu.VMEM, pltpu.SemaphoreType.DMA
    anywhere = pl.BlockSpec(memory_space=pl.ANY)
    shapes = [((48, 24, 256), BF), ((12, 96, 128), BF), ((48, 96), F32), ((9, 48, 96), F32)]
    results = pl.pallas_call(
        kernel,
        out_shape=tuple(vmem(*shape) for shape in shapes),
        in_specs=[anywhere] * 8,
        out_specs=(anywhere,) * 2 + (pl.BlockSpec(memory_space=pltpu.VMEM),) * 2,
        scratch_shapes=[
            vmem((48, 24, 256), BF),
            vmem((12, 96, 128), BF),
            vmem((9, 48, 48), BF),
            vmem((9, 96, 96), BF),
            vmem((48, 96), BF),
            vmem((9, 48, 96), BF),
            vmem((48, 24, 256), BF),
            vmem((12, 96, 128), BF),
            dma((8,)),
            dma((4,)),
            vmem((3, 144, 240), BF),
            vmem((288, 384), BF),
            vmem((96, 432), BF),
            vmem((1184, 128), BF),
            vmem((24, 48, 256), BF),
            vmem((27 * 48, 512), BF),
            vmem((25 * 48, 384), BF),
            vmem((8, 176, 128), BF),
            vmem((14, 8, 16, 128), BF),
            vmem((6, 96, 256), BF),
            vmem((1152, 256), BF),
            vmem((1152, 256), BF),
            vmem((48, 24, 256), BF),
            vmem((12, 96, 128), BF),
            vmem((8, 16, 128), BF),
            vmem((8, 16, 128), BF),
            vmem((3, 48, 256), BF),
            vmem((NB, 24, 128), BF),
            vmem((NB, 24, 128), BF),
            vmem((NA, 24, 128), BF),
            vmem((NB, 24, 128), BF),
            pltpu.SemaphoreType.REGULAR((2,)),
            dma((2, NC)),
            dma((2, NC)),
            dma((2,)),
            dma((2, NC)),
            dma((2,)),
            dma((2,)),
            dma((3, 16)),
            dma((3, 16)),
        ],
        compiler_params=pltpu.CompilerParams(
            collective_id=0, has_side_effects=True, vmem_limit_bytes=40 << 20
        ),
    )(
        *[
            pltpu.with_memory_space_constraint(array, pltpu.HBM)
            for array in (
                fine_in,
                coarse_in,
                fine_kernel,
                coarse_kernel,
                up_weight,
                jnp.swapaxes(down_weight, 1, 2),
                fine_cotangent,
                jnp.swapaxes(coarse_cotangent, 0, 1),
            )
        ]
    )
    joined_fine, joined_coarse, grad_up, grad_down = pl.pallas_call(
        write_out,
        out_shape=tuple(pltpu.HBM(*shape) for shape in shapes),
        in_specs=[anywhere] * 4,
        out_specs=(anywhere,) * 4,
        scratch_shapes=[dma((4,))],
    )(*[pltpu.with_memory_space_constraint(array, pltpu.VMEM) for array in results])
    return joined_fine, jnp.swapaxes(joined_coarse, 0, 1), grad_up, jnp.swapaxes(grad_down, 1, 2)


def solution(mesh):
    strips = P(None, ("rows", "ch"), None)
    return jax.shard_map(
        shards,
        mesh=mesh,
        in_specs=(strips, P("ch", "rows", None), P(), P(), P(), P(), strips, strips),
        out_specs=(strips, strips, P(), P()),
        check_vma=False,
    )
```
